256 devices in a mesh: wide: 32 (over x, y, core), narrow: 8 (over z).
Axes of the slice: x: 4, y: 4, z: 8, core: 2. Of those that a mesh axis runs over, the one named last changes fastest.
Arguments:
- inputs: bfloat16 [65536, 8192], P('wide', 'narrow'), may hold values from -6 to 6
- cotangent: bfloat16 [65536, 1024], P('wide'), may hold values from -6 to 6
- value_matrix: bfloat16 [8192, 1024], P('narrow', 'wide'), may hold values from -0.0625 to 0.0625
- adapter_down_maps: bfloat16 [32, 8192, 64], P('wide', 'narrow'), may hold values from -0.0625 to 0.0625
- adapter_up_maps: bfloat16 [32, 64, 1024], P('wide', None, 'narrow'), may hold values from -0.1875 to 0.1875
- task_of_block: int32 [512, 1], P('wide'), may hold values from 0 to 31; in each aligned block of 16 rows (0 to 15, 16 to 31, ...) no two rows name the same one
- valid_block_rows: int32 [512], P('wide'), may hold values from 1 to 128
- adapter_of_task: int32 [32], replicated, may hold values from 0 to 31, each once
Outputs:
- input_gradient: bfloat16 [65536, 8192], P('wide', 'narrow')
- down_grad: float32 [32, 8192, 64], P('wide', 'narrow')
- up_grad: float32 [32, 64, 1024], P('wide', None, 'narrow')
The draws below stay inside these ranges and needn't reach their ends.
Inputs may be any that keep to these rules, and one draw needn't show every extreme that they name: `task_of_block`: among the 16 blocks of one index of wide (aligned runs of blocks) no task appears more than 1 times. `adapter_of_task`: each adapter serves exactly one task.
All inputs are finite; a program needn't handle non-finite values.
Results may differ from the reference program's by a relative error of at most 0.0039.
Values may be sent and summed in bfloat16 or wider, within the bound.
No kernel may reach another device: no remote copies, remote signals or barrier semaphores. Data moves between devices by JAX's collectives and lax.ppermute only.
A program may use at most 128 MiB of HBM per device.

```python
import math
import jax
import jax.numpy as jnp
import numpy as np
from jax import lax

MODEL_WIDTH = 8192
VALUE_FEATURES = 1024
ADAPTER_RANK = 64
BLOCK_ROWS = 128
BLK_DEV = 16
BLOCKS = 512
TOKENS = 65536
ADAPTER_COUNT = 32
TASKS = 32
CAP = 1


def touch_ends(result, key, smallest, top_value):
    place = [jax.random.randint(jax.random.fold_in(key, axis), (), 0, length) for axis, length in enumerate(result.shape)]
    widest = result.shape.index(max(result.shape))
    beside = place[:widest] + [(place[widest] + 1) % result.shape[widest]] + place[widest + 1:]
    return result.at[tuple(place)].set(smallest).at[tuple(beside)].set(top_value)


def level_of(own_key, shape, pieces, smallest, top_value):
    factor_of = 1.0
    for dim, blocks in pieces:
        draws = jax.random.uniform(jax.random.fold_in(jax.random.fold_in(own_key, 6), dim), (blocks,), jnp.float32, smallest / len(pieces), top_value / len(pieces))
        factor_of = factor_of * jnp.repeat(jnp.exp(draws), shape[dim] // blocks).reshape((-1,) + (1,) * (len(shape) - 1 - dim))
    return factor_of


def assign_block(own_key, own, number, rows, number_of, top, most, lean):
    order = jax.random.permutation(own_key, number_of)
    heavy_load, common = shares(number_of, rows * top, most, lean, True), shares(number_of, rows * top, most, lean, False)
    places = jnp.arange(number_of)

    def named(sizes, turn):
        used = int((sizes > 0).sum())
        fixed = max(1, used // 4)
        passed = fixed + (places - fixed + turn * (used - fixed)) % max(1, number_of - fixed)
        return jnp.zeros((number_of,), jnp.int32).at[order[jnp.where(places < fixed, places, passed)]].set(jnp.asarray(sizes, jnp.int32))

    sizes = jnp.where(number % 4 == 0, named(heavy_load, number // 4), named(common, number - number // 4 - 1))
    mixed = jax.random.permutation(jax.random.fold_in(own, 3), number_of)
    donor, receiver = mixed[0:number_of // 2 * 2:2], mixed[1:number_of // 2 * 2:2]
    margin = jnp.minimum(sizes[donor] - 1, most - sizes[receiver]) // 2
    margin = jnp.where((donor == order[0]) | (receiver == order[0]) | (sizes[receiver] == 0), 0, jnp.maximum(margin, 0))
    passed = jax.random.randint(jax.random.fold_in(own, 4), (number_of // 2,), 0, 1 << 20) % (margin + 1)
    sizes = sizes.at[donor].add(-passed).at[receiver].add(passed)
    labels = jnp.searchsorted(jnp.cumsum(sizes), jnp.arange(rows * top), side="right").astype(jnp.int32)
    listing = labels.reshape(top, rows).T
    listing = listing[jax.random.permutation(jax.random.fold_in(own, 1), rows)]
    turn = jax.random.randint(jax.random.fold_in(own, 2), (rows, 1), 0, top)
    return jnp.take_along_axis(listing, (jnp.arange(top)[None, :] + turn) % top, axis=1)


def shares(amount, total, most, skew, full):
    portions = [(1 << 20) // math.isqrt(grade ** skew) + 1 for grade in range(1, amount + 1)]
    largest = most if full else min(most, max(-(-total // amount), total * portions[0] // sum(portions)))
    least = 1 if total - largest >= amount - 1 else 0
    given, surplus = [largest] + [least] * (amount - 1), total - largest - least * (amount - 1)
    while surplus > 0:
        candidates = [i for i in range(1, amount) if given[i] < largest] or [i for i in range(1, amount) if given[i] < most]
        mass, left = sum([portions[i] for i in candidates]), surplus
        for i in candidates:
            addition = min(most - given[i], max(1, left * portions[i] // mass), surplus)
            given[i] = given[i] + addition
            surplus = surplus - addition
    return np.array(given)


def normal_values(own_key, shape, scale, limit, pieces=(), kind=jnp.bfloat16):
    gain = level_of(own_key, shape, pieces, -0.22, 0.18) if pieces else 1.0
    result = jax.random.normal(own_key, shape, jnp.float32) * scale * gain
    return jnp.minimum(jnp.maximum(result, -limit), limit).astype(kind)


def setup_inputs(seed: int = 0) -> dict:
    seeds = jax.random.split(jax.random.key(seed), 9)
    inputs = normal_values(seeds[0], (TOKENS, MODEL_WIDTH), 1.0, 6.0, ((0, 32), (1, 8)))
    cotangent = normal_values(seeds[1], (TOKENS, VALUE_FEATURES), 1.0, 6.0, ((0, 32),))
    value_matrix = normal_values(seeds[2], (MODEL_WIDTH, VALUE_FEATURES), MODEL_WIDTH ** -0.5, 0.0625, ((0, 8), (1, 32)))
    adapter_down_maps = normal_values(seeds[3], (ADAPTER_COUNT, MODEL_WIDTH, ADAPTER_RANK), MODEL_WIDTH ** -0.5, 0.0625, ((0, 32), (1, 8)))
    adapter_up_maps = normal_values(seeds[4], (ADAPTER_COUNT, ADAPTER_RANK, VALUE_FEATURES), VALUE_FEATURES ** -0.5, 0.1875, ((0, 32), (2, 8)))
    task_of_block_keys = jax.random.split(jax.random.fold_in(seeds[5], 1), BLOCKS // BLK_DEV)
    task_of_block_turns = jax.random.permutation(jax.random.fold_in(seeds[5], 3), BLOCKS // BLK_DEV)
    task_of_block = jax.vmap(lambda own, number: assign_block(jax.random.fold_in(seeds[5], 2), own, number, BLK_DEV, TASKS, 1, CAP, 2))(task_of_block_keys, task_of_block_turns).reshape((BLOCKS, 1))
    valid_block_rows = touch_ends(jax.random.randint(seeds[6], (BLOCKS,), 1, BLOCK_ROWS + 1), jax.random.fold_in(seeds[6], 1), 1, BLOCK_ROWS).astype(jnp.int32)
    adapter_of_task = jax.random.permutation(seeds[7], ADAPTER_COUNT).astype(jnp.int32)
    return dict(inputs=inputs, cotangent=cotangent, value_matrix=value_matrix, adapter_down_maps=adapter_down_maps, adapter_up_maps=adapter_up_maps, task_of_block=task_of_block, valid_block_rows=valid_block_rows, adapter_of_task=adapter_of_task)


ADAPTER_SCALE = 2.0


def matrix_product(left, right):
    return jnp.dot(left, right, preferred_element_type=jnp.float32)


def reference(inputs, cotangent, value_matrix, adapter_down_maps, adapter_up_maps, task_of_block, valid_block_rows, adapter_of_task):
    x_blocks = inputs.reshape(BLOCKS, BLOCK_ROWS, MODEL_WIDTH)
    g_blocks = cotangent.reshape(BLOCKS, BLOCK_ROWS, VALUE_FEATURES)
    adapter_of = adapter_of_task[task_of_block[:, 0].astype(jnp.int32)].astype(jnp.int32)
    row_index = jnp.arange(BLOCK_ROWS, dtype=jnp.int32)

    def block_step(totals, item):
        down_total, up_sum_total = totals
        x_block, g_block, valid, adapter_pick = item
        live = (row_index < valid)[:, None]
        masked_rows = jnp.where(live, g_block, jnp.zeros((), g_block.dtype))
        down_matrix = lax.dynamic_index_in_dim(adapter_down_maps, adapter_pick, 0, keepdims=False)
        up_matrix = lax.dynamic_index_in_dim(adapter_up_maps, adapter_pick, 0, keepdims=False)
        low_rank_grad = matrix_product(x_block, down_matrix).astype(jnp.bfloat16)
        backward_grad = (ADAPTER_SCALE * matrix_product(masked_rows, up_matrix.T)).astype(jnp.bfloat16)
        adapter_term = matrix_product(backward_grad, down_matrix.T).astype(jnp.bfloat16)
        frozen_grad = matrix_product(masked_rows, value_matrix.T)
        gradient_rows = (frozen_grad + adapter_term.astype(jnp.float32)).astype(jnp.bfloat16)
        down_total = down_total.at[adapter_pick].add(matrix_product(x_block.T, backward_grad))
        up_sum_total = up_sum_total.at[adapter_pick].add(ADAPTER_SCALE * matrix_product(low_rank_grad.T, masked_rows))
        return (down_total, up_sum_total), gradient_rows

    start = (jnp.zeros((ADAPTER_COUNT, MODEL_WIDTH, ADAPTER_RANK), jnp.float32), jnp.zeros((ADAPTER_COUNT, ADAPTER_RANK, VALUE_FEATURES), jnp.float32))
    (down_grad, up_grad), rows_out = lax.scan(block_step, start, (x_blocks, g_blocks, valid_block_rows, adapter_of))
    return rows_out.reshape(TOKENS, MODEL_WIDTH), down_grad, up_grad
```

```python
import functools

import jax
import jax.numpy as jnp
from jax import lax
from jax.experimental import pallas as pl
from jax.experimental.pallas import tpu as pltpu
from jax.sharding import PartitionSpec as P

BLOCK_ROWS = 128
ADAPTER_SCALE = 2.0
RANK = 64
SIDE = 4
NBLK = 16
OWNERS = 32
DEPTH = 8
HALF = NBLK // 2
VMEM_LIMIT = 48 * 1024 * 1024

NT = (((1,), (1,)), ((), ()))
TN = (((0,), (0,)), ((), ()))

SLOT_IN, SLOT_OUT, VALID, PLACE, ORDER, SCALARS = 0, 16, 32, 48, 64, 96


def wide_index(x, y, c):
    return ((x % SIDE) * SIDE + (y % SIDE)) * 2 + c


def short_axis(d):
    return [
        (wide_index(x, y, c), wide_index(x + d, y, c) if c == 0 else wide_index(x, y + d, c))
        for x in range(SIDE)
        for y in range(SIDE)
        for c in range(2)
    ]


def long_axis(d):
    return [
        (wide_index(x, y, c), wide_index(x, y + d, c) if c == 0 else wide_index(x + d, y, c))
        for x in range(SIDE)
        for y in range(SIDE)
        for c in range(2)
    ]


def swap_cores(v):
    return lax.ppermute(v, "wide", [(w, w ^ 1) for w in range(OWNERS)])


def shift(v, axis, d):
    return lax.ppermute(v, "wide", axis(d))


def gather_first(own):
    got = {d: shift(own, short_axis, d) for d in (1, 3, 2)}
    return jnp.concatenate([own, got[1], got[2], got[3]], axis=0)


def gather_second(line):
    got = {d: shift(line, long_axis, d) for d in (1, 3, 2)}
    return [line, got[1], got[2], got[3]]


def reduce_to_owner(keep, give):
    got = swap_cores(give)
    rows = keep.shape[0] // SIDE
    piece = rows // SIDE

    def merged(i):
        part = slice(i * rows, (i + 1) * rows)
        return keep[part].astype(jnp.float32) + got[part].astype(jnp.float32)

    lines = [shift(merged(d).astype(jnp.bfloat16), long_axis, d) for d in (1, 3, 2)]
    line = merged(0)
    for other in lines:
        line = line + other.astype(jnp.float32)
    parts = [
        shift(line[d * piece : (d + 1) * piece].astype(jnp.bfloat16), short_axis, d)
        for d in (1, 3, 2)
    ]
    total = line[:piece]
    for other in parts:
        total = total + other.astype(jnp.float32)
    return total


def narrow_send(v, f):
    return lax.ppermute(v, "narrow", [(i, f(i) % DEPTH) for i in range(DEPTH)])


def reduce_narrow(keep, give, scale):
    total = keep + narrow_send(give, lambda i: i ^ 1).astype(jnp.float32)
    small = total.astype(jnp.bfloat16)
    for d in (2, 6, 4):
        total = total + narrow_send(small, lambda i, d=d: i + d).astype(jnp.float32)
    mine = (scale * total).astype(jnp.bfloat16)
    return mine, narrow_send(mine, lambda i: i ^ 1)


def back_kernel(s_ref, g_ref, b0_ref, b1_ref, keep_ref, give_ref, maps):
    maps[0 : NBLK * RANK, :] = b0_ref[...]
    maps[NBLK * RANK :, :] = b1_ref[...]
    first = s_ref[PLACE + 1] * HALF
    lane = lax.broadcasted_iota(jnp.int32, (RANK, BLOCK_ROWS), 1)
    for t in range(NBLK):
        b = lax.rem(first + t, NBLK)
        up = maps[pl.ds(pl.multiple_of(s_ref[SLOT_IN + b] * RANK, RANK), RANK), :]
        g = g_ref[pl.ds(pl.multiple_of(b * BLOCK_ROWS, BLOCK_ROWS), BLOCK_ROWS), :]
        r = lax.dot_general(up, g, NT, preferred_element_type=jnp.float32)
        r = jnp.where(lane < s_ref[VALID + b], r, 0.0)
        at = slice((t % HALF) * BLOCK_ROWS, (t % HALF + 1) * BLOCK_ROWS)
        if t < HALF:
            keep_ref[:, at] = r
        else:
            give_ref[:, at] = r.astype(jnp.bfloat16)


def back_part(scalars, cotangent, b0, b1):
    rows = cotangent.shape[0]
    width = b0.shape[1]
    return pl.pallas_call(
        back_kernel,
        grid_spec=pltpu.PrefetchScalarGridSpec(
            num_scalar_prefetch=1,
            grid=(1,),
            in_specs=[
                pl.BlockSpec((rows, width), lambda i, s: (0, s[PLACE])),
                pl.BlockSpec(b0.shape, lambda i, s: (0, 0)),
                pl.BlockSpec(b1.shape, lambda i, s: (0, 0)),
            ],
            out_specs=[pl.BlockSpec((RANK, rows // 2), lambda i, s: (0, 0))] * 2,
            scratch_shapes=[pltpu.VMEM((OWNERS * RANK, width), jnp.bfloat16)],
        ),
        out_shape=[
            jax.ShapeDtypeStruct((RANK, rows // 2), jnp.float32),
            jax.ShapeDtypeStruct((RANK, rows // 2), jnp.bfloat16),
        ],
        compiler_params=pltpu.CompilerParams(vmem_limit_bytes=VMEM_LIMIT),
        cost_estimate=pl.CostEstimate(
            flops=2 * rows * RANK * width, bytes_accessed=2 * 2**20, transcendentals=0
        ),
        name="back_part",
    )(scalars, cotangent, b0, b1)


def low_kernel(s_ref, x_ref, *refs):
    pieces, (keep_ref, give_ref, xs, maps, sem_a, sem_x) = refs[:8], refs[8:]
    per = pieces[0].shape[0]
    first = s_ref[PLACE + 1] * HALF
    loads = [
        pltpu.make_async_copy(p, maps.at[pl.ds(k * per, per), :], sem_a.at[k])
        for k, p in enumerate(pieces)
    ]
    blocks = []
    for t in range(NBLK):
        b = lax.rem(first + t, NBLK)
        at = pl.ds(pl.multiple_of(b * BLOCK_ROWS, BLOCK_ROWS), BLOCK_ROWS)
        to = pl.ds(t * BLOCK_ROWS, BLOCK_ROWS)
        blocks.append(pltpu.make_async_copy(x_ref.at[at, :], xs.at[to, :], sem_x.at[t]))
    for copy in loads + blocks:
        copy.start()
    for copy in loads:
        copy.wait()
    for t in range(NBLK):
        b = lax.rem(first + t, NBLK)
        blocks[t].wait()
        down = maps[pl.ds(pl.multiple_of(s_ref[SLOT_IN + b] * RANK, RANK), RANK), :]
        x = xs[t * BLOCK_ROWS : (t + 1) * BLOCK_ROWS, :]
        r = lax.dot_general(down, x, NT, preferred_element_type=jnp.float32)
        at = slice((t % HALF) * BLOCK_ROWS, (t % HALF + 1) * BLOCK_ROWS)
        if t < HALF:
            keep_ref[:, at] = r
        else:
            give_ref[:, at] = r.astype(jnp.bfloat16)


def low_part(scalars, x, pieces):
    rows, width = x.shape
    hbm = pl.BlockSpec(memory_space=pl.ANY)
    return pl.pallas_call(
        low_kernel,
        grid_spec=pltpu.PrefetchScalarGridSpec(
            num_scalar_prefetch=1,
            grid=(1,),
            in_specs=[hbm] * 9,
            out_specs=[pl.BlockSpec((RANK, rows // 2), lambda i, s: (0, 0))] * 2,
            scratch_shapes=[
                pltpu.VMEM((rows, width), jnp.bfloat16),
                pltpu.VMEM((OWNERS * RANK, width), jnp.bfloat16),
                pltpu.SemaphoreType.DMA((8,)),
                pltpu.SemaphoreType.DMA((NBLK,)),
            ],
        ),
        out_shape=[
            jax.ShapeDtypeStruct((RANK, rows // 2), jnp.float32),
            jax.ShapeDtypeStruct((RANK, rows // 2), jnp.bfloat16),
        ],
        compiler_params=pltpu.CompilerParams(vmem_limit_bytes=VMEM_LIMIT),
        cost_estimate=pl.CostEstimate(
            flops=2 * rows * RANK * width, bytes_accessed=8 * 2**20, transcendentals=0
        ),
        name="low_part",
    )(scalars, x, *pieces)


def down_kernel(s_ref, x_ref, mine_ref, other_ref, keep_ref, give_ref, xs, acc, sem_x, sem_o):
    first = s_ref[PLACE + 1] * HALF
    half_rows = NBLK * RANK
    blocks = []
    for t in range(NBLK):
        b = lax.rem(first + t, NBLK)
        at = pl.ds(pl.multiple_of(b * BLOCK_ROWS, BLOCK_ROWS), BLOCK_ROWS)
        to = pl.ds(t * BLOCK_ROWS, BLOCK_ROWS)
        blocks.append(pltpu.make_async_copy(x_ref.at[at, :], xs.at[to, :], sem_x.at[t]))
    for copy in blocks:
        copy.start()
    acc[...] = jnp.zeros_like(acc)
    for t in range(NBLK):
        b = lax.rem(first + t, NBLK)
        blocks[t].wait()
        at = slice((t % HALF) * BLOCK_ROWS, (t % HALF + 1) * BLOCK_ROWS)
        back = (mine_ref if t < HALF else other_ref)[:, at]
        x = xs[t * BLOCK_ROWS : (t + 1) * BLOCK_ROWS, :]
        r = jnp.dot(back, x, preferred_element_type=jnp.float32)
        slot = pl.ds(pl.multiple_of(s_ref[SLOT_OUT + b] * RANK, RANK), RANK)
        acc[slot, :] = r.astype(jnp.bfloat16)
    outs = [
        pltpu.make_async_copy(acc.at[pl.ds(half_rows, half_rows), :], give_ref, sem_o.at[0]),
        pltpu.make_async_copy(acc.at[pl.ds(0, half_rows), :], keep_ref, sem_o.at[1]),
    ]
    for copy in outs:
        copy.start()
    for copy in outs:
        copy.wait()


def down_part(scalars, x, mine, other):
    rows, width = x.shape
    hbm = pl.BlockSpec(memory_space=pl.ANY)
    half = pl.BlockSpec(mine.shape, lambda i, s: (0, 0))
    out = jax.ShapeDtypeStruct((NBLK * RANK, width), jnp.bfloat16)
    return pl.pallas_call(
        down_kernel,
        grid_spec=pltpu.PrefetchScalarGridSpec(
            num_scalar_prefetch=1,
            grid=(1,),
            in_specs=[hbm, half, half],
            out_specs=[hbm, hbm],
            scratch_shapes=[
                pltpu.VMEM((rows, width), jnp.bfloat16),
                pltpu.VMEM((OWNERS * RANK, width), jnp.bfloat16),
                pltpu.SemaphoreType.DMA((NBLK,)),
                pltpu.SemaphoreType.DMA((2,)),
            ],
        ),
        out_shape=[out, out],
        compiler_params=pltpu.CompilerParams(vmem_limit_bytes=VMEM_LIMIT),
        cost_estimate=pl.CostEstimate(
            flops=2 * rows * RANK * width, bytes_accessed=8 * 2**20, transcendentals=0
        ),
        name="down_part",
    )(scalars, x, mine, other)


def up_kernel(s_ref, g_ref, mine_ref, other_ref, keep_ref, give_ref, acc):
    first = s_ref[PLACE + 1] * HALF
    lane = lax.broadcasted_iota(jnp.int32, (RANK, BLOCK_ROWS), 1)
    acc[...] = jnp.zeros_like(acc)
    for t in range(NBLK):
        b = lax.rem(first + t, NBLK)
        at = slice((t % HALF) * BLOCK_ROWS, (t % HALF + 1) * BLOCK_ROWS)
        low = (mine_ref if t < HALF else other_ref)[:, at]
        low = jnp.where(lane < s_ref[VALID + b], low.astype(jnp.float32), 0.0).astype(jnp.bfloat16)
        g = g_ref[pl.ds(pl.multiple_of(b * BLOCK_ROWS, BLOCK_ROWS), BLOCK_ROWS), :]
        r = ADAPTER_SCALE * jnp.dot(low, g, preferred_element_type=jnp.float32)
        slot = pl.ds(pl.multiple_of(s_ref[SLOT_OUT + b] * RANK, RANK), RANK)
        acc[slot, :] = r.astype(jnp.bfloat16)
    keep_ref[...] = acc[: NBLK * RANK, :]
    give_ref[...] = acc[NBLK * RANK :, :]


def up_part(scalars, cotangent, mine, other, width):
    rows = cotangent.shape[0]
    half = pl.BlockSpec(mine.shape, lambda i, s: (0, 0))
    out = jax.ShapeDtypeStruct((NBLK * RANK, width), jnp.bfloat16)
    return pl.pallas_call(
        up_kernel,
        grid_spec=pltpu.PrefetchScalarGridSpec(
            num_scalar_prefetch=1,
            grid=(1,),
            in_specs=[pl.BlockSpec((rows, width), lambda i, s: (0, s[PLACE])), half, half],
            out_specs=[pl.BlockSpec((NBLK * RANK, width), lambda i, s: (0, 0))] * 2,
            scratch_shapes=[pltpu.VMEM((OWNERS * RANK, width), jnp.bfloat16)],
        ),
        out_shape=[out, out],
        compiler_params=pltpu.CompilerParams(vmem_limit_bytes=VMEM_LIMIT),
        cost_estimate=pl.CostEstimate(
            flops=2 * rows * RANK * width, bytes_accessed=2 * 2**20, transcendentals=0
        ),
        name="up_part",
    )(scalars, cotangent, mine, other)


def input_kernel(s_ref, g_ref, mine_ref, other_ref, *refs):
    v_pieces, a_pieces = refs[:8], refs[8:16]
    out_ref, gs, vs, maps, outs, sem_g, sem_v, sem_a, sem_o = refs[16:]
    first = s_ref[PLACE + 1] * HALF
    features = vs.shape[0]
    share = features // OWNERS
    per = a_pieces[0].shape[0]
    loads_v = []
    for k in range(OWNERS):
        to = pl.ds(pl.multiple_of(s_ref[ORDER + k] * share, share), share)
        src = v_pieces[k // SIDE].at[pl.ds((k % SIDE) * share, share), :]
        loads_v.append(pltpu.make_async_copy(src, vs.at[to, :], sem_v.at[k]))
    loads_a = [
        pltpu.make_async_copy(p, maps.at[pl.ds(k * per, per), :], sem_a.at[k])
        for k, p in enumerate(a_pieces)
    ]
    step = 2 * BLOCK_ROWS
    loads_g, stores = [], []
    for t in range(HALF):
        b = lax.rem(first + 2 * t, NBLK)
        at = pl.ds(pl.multiple_of(b * BLOCK_ROWS, step), step)
        to = pl.ds(t * step, step)
        loads_g.append(pltpu.make_async_copy(g_ref.at[at, :], gs.at[to, :], sem_g.at[t]))
        stores.append(pltpu.make_async_copy(outs.at[to, :], out_ref.at[at, :], sem_o.at[t]))
    for copy in loads_v + loads_g[:1] + loads_a + loads_g[1:]:
        copy.start()
    for copy in loads_v:
        copy.wait()
    row = lax.broadcasted_iota(jnp.int32, (BLOCK_ROWS, features), 0)
    for t in range(HALF):
        loads_g[t].wait()
        if t == 0:
            for copy in loads_a:
                copy.wait()
        lives, terms = [], []
        for u in range(2):
            k = 2 * t + u
            b = lax.rem(first + k, NBLK)
            g = gs[k * BLOCK_ROWS : (k + 1) * BLOCK_ROWS, :]
            lives.append(jnp.where(row < s_ref[VALID + b], g, jnp.zeros_like(g)))
            at = slice((k % HALF) * BLOCK_ROWS, (k % HALF + 1) * BLOCK_ROWS)
            back = (mine_ref if k < HALF else other_ref)[:, at]
            down = maps[pl.ds(pl.multiple_of(s_ref[SLOT_IN + b] * RANK, RANK), RANK), :]
            term = lax.dot_general(back, down, TN, preferred_element_type=jnp.float32)
            terms.append(term.astype(jnp.bfloat16).astype(jnp.float32))
        live = jnp.concatenate(lives, axis=0)
        frozen = jnp.dot(live, vs[...], preferred_element_type=jnp.float32)
        for u in range(2):
            k = 2 * t + u
            outs[k * BLOCK_ROWS : (k + 1) * BLOCK_ROWS, :] = (
                frozen[u * BLOCK_ROWS : (u + 1) * BLOCK_ROWS] + terms[u]
            ).astype(jnp.bfloat16)
        stores[t].start()
    for copy in stores:
        copy.wait()


def input_part(scalars, cotangent, mine, other, v_pieces, a_pieces):
    rows, features = cotangent.shape
    width = v_pieces[0].shape[1]
    hbm = pl.BlockSpec(memory_space=pl.ANY)
    half = pl.BlockSpec(mine.shape, lambda i, s: (0, 0))
    return pl.pallas_call(
        input_kernel,
        grid_spec=pltpu.PrefetchScalarGridSpec(
            num_scalar_prefetch=1,
            grid=(1,),
            in_specs=[hbm, half, half] + [hbm] * 16,
            out_specs=hbm,
            scratch_shapes=[
                pltpu.VMEM((rows, features), jnp.bfloat16),
                pltpu.VMEM((features, width), jnp.bfloat16),
                pltpu.VMEM((OWNERS * RANK, width), jnp.bfloat16),
                pltpu.VMEM((rows, width), jnp.bfloat16),
                pltpu.SemaphoreType.DMA((HALF,)),
                pltpu.SemaphoreType.DMA((OWNERS,)),
                pltpu.SemaphoreType.DMA((8,)),
                pltpu.SemaphoreType.DMA((HALF,)),
            ],
        ),
        out_shape=jax.ShapeDtypeStruct((rows, width), jnp.bfloat16),
        compiler_params=pltpu.CompilerParams(vmem_limit_bytes=VMEM_LIMIT),
        cost_estimate=pl.CostEstimate(
            flops=2 * rows * features * width, bytes_accessed=14 * 2**20, transcendentals=0
        ),
        name="input_part",
    )(scalars, cotangent, mine, other, *v_pieces, *a_pieces)


def make_scalars(task_of_block, valid_block_rows, adapter_of_task):
    w = lax.axis_index("wide")
    n = lax.axis_index("narrow")
    x, y, c = w // (2 * SIDE), (w // 2) % SIDE, w % 2
    hit = task_of_block == lax.broadcasted_iota(jnp.int32, (NBLK, OWNERS), 1)
    owner = jnp.sum(jnp.where(hit, adapter_of_task[None, :], 0), axis=1)
    ox, oy, oc = owner // (2 * SIDE), (owner // 2) % SIDE, owner % 2
    dx, dy = (x - ox) % SIDE, (y - oy) % SIDE
    i, j = jnp.where(oc == 0, dy, dx), jnp.where(oc == 0, dx, dy)
    side = (oc + c) % 2 * (SIDE * SIDE)
    slot_in = side + i * SIDE + j
    slot_out = side + (-i) % SIDE * SIDE + (-j) % SIDE
    k = lax.broadcasted_iota(jnp.int32, (OWNERS, 1), 0)[:, 0]
    kc = (k // (SIDE * SIDE) + c) % 2
    ki, kj = (k // SIDE) % SIDE, k % SIDE
    kx = (x - jnp.where(kc == 0, kj, ki)) % SIDE
    ky = (y - jnp.where(kc == 0, ki, kj)) % SIDE
    order = (kx * SIDE + ky) * 2 + kc
    spot = lax.broadcasted_iota(jnp.int32, (NBLK, 1), 0)[:, 0]
    place = jnp.where(spot == 0, n, n % 2)
    return jnp.concatenate([slot_in, slot_out, valid_block_rows, place, order])


def body(
    inputs,
    cotangent,
    value_matrix,
    adapter_down_maps,
    adapter_up_maps,
    task_of_block,
    valid_block_rows,
    adapter_of_task,
):
    scalars = make_scalars(task_of_block, valid_block_rows, adapter_of_task)
    up_own = adapter_up_maps[0]
    down_own = adapter_down_maps[0].T
    value_own = value_matrix.T

    up_line = gather_first(up_own)
    up_same = jnp.concatenate(gather_second(up_line), axis=0)
    up_sibling = swap_cores(up_same)
    keep, give = back_part(scalars, cotangent, up_same, up_sibling)
    back_mine, back_other = reduce_narrow(keep, give, ADAPTER_SCALE)

    down_pieces = gather_second(gather_first(down_own))
    down_pieces = down_pieces + [swap_cores(p) for p in down_pieces]
    keep, give = low_part(scalars, inputs, down_pieces)
    low_mine, low_other = reduce_narrow(keep, give, 1.0)

    value_pieces = gather_second(gather_first(value_own))
    value_pieces = value_pieces + [swap_cores(p) for p in value_pieces]

    down_grad = reduce_to_owner(*down_part(scalars, inputs, back_mine, back_other))
    up_grad = reduce_to_owner(
        *up_part(scalars, cotangent, low_mine, low_other, up_own.shape[1])
    )
    input_gradient = input_part(
        scalars, cotangent, back_mine, back_other, value_pieces, down_pieces
    )
    return input_gradient, down_grad.T[None], up_grad[None]


def solution(mesh):
    return jax.shard_map(
        body,
        mesh=mesh,
        in_specs=(
            P("wide", "narrow"),
            P("wide", None),
            P("narrow", "wide"),
            P("wide", "narrow", None),
            P("wide", None, "narrow"),
            P("wide", None),
            P("wide"),
            P(),
        ),
        out_specs=(P("wide", "narrow"), P("wide", "narrow", None), P("wide", None, "narrow")),
        check_vma=False,
    )
```

```python
import jax
import jax.numpy as jnp
from jax import lax
from jax.experimental import pallas as pl
from jax.experimental.pallas import tpu as pltpu
from jax.sharding import PartitionSpec as P

BLOCK_ROWS = 128
ADAPTER_SCALE = 2.0
RANK = 64
SIDE = 4
NBLK = 16
OWNERS = 32
DEPTH = 8
HALF = NBLK // 2
VMEM_LIMIT = 48 * 1024 * 1024

SMALL = pl.CostEstimate(flops=1, bytes_accessed=1, transcendentals=0)

NT = (((1,), (1,)), ((), ()))
TN = (((0,), (0,)), ((), ()))

SLOT_IN, SLOT_OUT, VALID, PLACE, ORDER, SCALARS = 0, 16, 32, 48, 64, 96


def wide_index(x, y, c):
    return ((x % SIDE) * SIDE + (y % SIDE)) * 2 + c


def short_axis(d):
    return [
        (wide_index(x, y, c), wide_index(x + d, y, c) if c == 0 else wide_index(x, y + d, c))
        for x in range(SIDE)
        for y in range(SIDE)
        for c in range(2)
    ]


def long_axis(d):
    return [
        (wide_index(x, y, c), wide_index(x, y + d, c) if c == 0 else wide_index(x + d, y, c))
        for x in range(SIDE)
        for y in range(SIDE)
        for c in range(2)
    ]


def swap_cores(v):
    return lax.ppermute(v, "wide", [(w, w ^ 1) for w in range(OWNERS)])


def tie(*values):
    return lax.optimization_barrier(values)


def shift(v, axis, d):
    return lax.ppermute(v, "wide", axis(d))


def unpack_kernel(own_ref, r1_ref, r2_ref, r3_ref, b_ref, v_ref):
    rows = own_ref.shape[0] - RANK
    for k, ref in enumerate((own_ref, r1_ref, r2_ref, r3_ref)):
        b_ref[k * RANK : (k + 1) * RANK, :] = ref[:RANK, :]
        v_ref[k * rows : (k + 1) * rows, :] = ref[RANK:, :]


def unpack(own, got):
    rows, width = own.shape
    return pl.pallas_call(
        unpack_kernel,
        out_shape=[
            jax.ShapeDtypeStruct((SIDE * RANK, width), jnp.bfloat16),
            jax.ShapeDtypeStruct((SIDE * (rows - RANK), width), jnp.bfloat16),
        ],
        cost_estimate=SMALL,
        name="unpack",
    )(own, got[1], got[2], got[3])


def gather_short(own):
    return {d: shift(own, short_axis, d) for d in (1, 3, 2)}


def gather_narrow(own):
    n = lax.axis_index("narrow")
    for q in (1, 2, 4):
        other = narrow_send(own, lambda i, q=q: i ^ q)
        late = (n // q) % 2 == 1
        own = jnp.concatenate(
            [jnp.where(late, other, own), jnp.where(late, own, other)], axis=1
        )
    return own


def gather_second(line):
    got = {d: shift(line, long_axis, d) for d in (1, 3, 2)}
    return [line, got[1], got[2], got[3]]


def merge_cores(keep, got):
    rows = keep.shape[0] // SIDE
    return [
        keep[i * rows : (i + 1) * rows].astype(jnp.float32)
        + got[i * rows : (i + 1) * rows].astype(jnp.float32)
        for i in range(SIDE)
    ]


def add_all(total, others):
    for other in others:
        total = total + other.astype(jnp.float32)
    return total


def reduce_short(down, up):
    piece = down.shape[0] // SIDE
    width, share = down.shape[1], up.shape[1]
    high = up.astype(jnp.bfloat16)
    rest = (up - high.astype(jnp.float32)).astype(jnp.bfloat16)
    line = jnp.concatenate([down.astype(jnp.bfloat16), high, rest], axis=1)
    got = [shift(line[d * piece : (d + 1) * piece], short_axis, d) for d in (1, 3, 2)]
    down_total = add_all(down[:piece], [g[:, :width] for g in got])
    up_total = add_all(up[:piece], [g[:, width : width + share] for g in got])
    return down_total, add_all(up_total, [g[:, width + share :] for g in got])


def narrow_send(v, f):
    return lax.ppermute(v, "narrow", [(i, f(i) % DEPTH) for i in range(DEPTH)])


def pair_step(v):
    return narrow_send(v, lambda i: i ^ 1)


def exchange(total, q):
    other = narrow_send(total.astype(jnp.bfloat16), lambda i: i ^ q)
    return total + other.astype(jnp.float32)


def block_at(b):
    return pl.ds(pl.multiple_of(b * BLOCK_ROWS, BLOCK_ROWS), BLOCK_ROWS)


def slot_at(slot):
    return pl.ds(pl.multiple_of(slot * RANK, RANK), RANK)


def back_kernel(s_ref, g_ref, x_ref, *refs):
    pieces, (back_ref, keep_ref, give_ref) = refs[:8], refs[8:11]
    gs, maps, xs, acc, sem_g, sem_b, sem_x, sem_o = refs[11:]
    per = pieces[0].shape[0]
    half_rows = NBLK * RANK
    loads = [
        pltpu.make_async_copy(p, maps.at[pl.ds(k * per, per), :], sem_b.at[k])
        for k, p in enumerate(pieces)
    ]
    g_loads, x_loads = [], []
    for t in range(HALF):
        at = pl.ds(2 * t * BLOCK_ROWS, 2 * BLOCK_ROWS)
        g_loads.append(pltpu.make_async_copy(g_ref.at[at, :], gs.at[at, :], sem_g.at[t]))
        x_loads.append(pltpu.make_async_copy(x_ref.at[at, :], xs.at[at, :], sem_x.at[t]))
    for copy in loads:
        copy.start()
    for t in range(HALF):
        g_loads[t].start()
        x_loads[t].start()
    acc[...] = jnp.zeros_like(acc)
    for copy in loads:
        copy.wait()
    lane = lax.broadcasted_iota(jnp.int32, (RANK, BLOCK_ROWS), 1)

    def backs(t):
        rows = slice(t * BLOCK_ROWS, (t + 2) * BLOCK_ROWS)
        ups = [maps[slot_at(s_ref[SLOT_IN + t + u]), :] for u in range(2)]
        pair = lax.dot_general(
            jnp.concatenate(ups, axis=0), gs[rows, :], NT, preferred_element_type=jnp.float32
        )
        parts = []
        for u in range(2):
            r = pair[u * RANK : (u + 1) * RANK, u * BLOCK_ROWS : (u + 1) * BLOCK_ROWS]
            r = jnp.where(lane < s_ref[VALID + t + u], ADAPTER_SCALE * r, 0.0)
            parts.append(r.astype(jnp.bfloat16))
        return parts

    def grads(t, parts):
        for u in range(2):
            b = t + u
            at = slice(b * BLOCK_ROWS, (b + 1) * BLOCK_ROWS)
            back_ref[:, at] = parts[u]
            grad = jnp.dot(parts[u], xs[at, :], preferred_element_type=jnp.float32)
            acc[slot_at(s_ref[SLOT_OUT + b]), :] = grad.astype(jnp.bfloat16)

    before = None
    for t in range(0, NBLK, 2):
        g_loads[t // 2].wait()
        if t:
            x_loads[t // 2 - 1].wait()
        parts = backs(t)
        if t:
            grads(t - 2, before)
        before = parts
    x_loads[HALF - 1].wait()
    grads(NBLK - 2, before)
    outs = [
        pltpu.make_async_copy(acc.at[pl.ds(half_rows, half_rows), :], give_ref, sem_o.at[0]),
        pltpu.make_async_copy(acc.at[pl.ds(0, half_rows), :], keep_ref, sem_o.at[1]),
    ]
    for copy in outs:
        copy.start()
    for copy in outs:
        copy.wait()


def back_part(scalars, cotangent, x, pieces):
    rows, features = cotangent.shape
    width = x.shape[1]
    hbm = pl.BlockSpec(memory_space=pl.ANY)
    out = jax.ShapeDtypeStruct((NBLK * RANK, width), jnp.bfloat16)
    return pl.pallas_call(
        back_kernel,
        grid_spec=pltpu.PrefetchScalarGridSpec(
            num_scalar_prefetch=1,
            grid=(1,),
            in_specs=[hbm] * 10,
            out_specs=[pl.BlockSpec((RANK, rows), lambda i, s: (0, 0)), hbm, hbm],
            scratch_shapes=[
                pltpu.VMEM((rows, features), jnp.bfloat16),
                pltpu.VMEM((OWNERS * RANK, features), jnp.bfloat16),
                pltpu.VMEM((rows, width), jnp.bfloat16),
                pltpu.VMEM((OWNERS * RANK, width), jnp.bfloat16),
                pltpu.SemaphoreType.DMA((HALF,)),
                pltpu.SemaphoreType.DMA((8,)),
                pltpu.SemaphoreType.DMA((HALF,)),
                pltpu.SemaphoreType.DMA((2,)),
            ],
        ),
        out_shape=[jax.ShapeDtypeStruct((RANK, rows), jnp.bfloat16), out, out],
        compiler_params=pltpu.CompilerParams(vmem_limit_bytes=VMEM_LIMIT),
        cost_estimate=pl.CostEstimate(
            flops=4 * rows * RANK * width, bytes_accessed=16 * 2**20, transcendentals=0
        ),
        name="back_part",
    )(scalars, cotangent, x, *pieces)


def low_kernel(s_ref, x_ref, *refs):
    pieces, (keep_ref, give_ref, picked_ref, xs, maps, sem_a, sem_x, sem_p) = refs[:8], refs[8:]
    per = pieces[0].shape[0]
    first = s_ref[PLACE + 1] * HALF
    loads = [
        pltpu.make_async_copy(p, maps.at[pl.ds(k * per, per), :], sem_a.at[k])
        for k, p in enumerate(pieces)
    ]
    blocks = []
    for t in range(NBLK):
        b = lax.rem(first + t, NBLK)
        at = pl.ds(pl.multiple_of(b * BLOCK_ROWS, BLOCK_ROWS), BLOCK_ROWS)
        to = pl.ds(t * BLOCK_ROWS, BLOCK_ROWS)
        blocks.append(pltpu.make_async_copy(x_ref.at[at, :], xs.at[to, :], sem_x.at[t]))
    for copy in loads + blocks:
        copy.start()
    for copy in loads:
        copy.wait()
    picks = []
    for b in range(NBLK):
        to = picked_ref.at[pl.ds(b * RANK, RANK), :]
        picks.append(
            pltpu.make_async_copy(maps.at[slot_at(s_ref[SLOT_IN + b]), :], to, sem_p.at[b])
        )
        picks[b].start()
    for t in range(0, NBLK, 2):
        if t % 4 == 0:
            for copy in blocks[t : t + 4]:
                copy.wait()
        downs = []
        for u in (t, t + 1):
            b = lax.rem(first + u, NBLK)
            downs.append(maps[slot_at(s_ref[SLOT_IN + b]), :])
        x = xs[t * BLOCK_ROWS : (t + 2) * BLOCK_ROWS, :]
        pair = lax.dot_general(
            jnp.concatenate(downs, axis=0), x, NT, preferred_element_type=jnp.float32
        )
        for u in range(2):
            r = pair[u * RANK : (u + 1) * RANK, u * BLOCK_ROWS : (u + 1) * BLOCK_ROWS]
            k = (t + u) % HALF
            at = slice(k * BLOCK_ROWS, (k + 1) * BLOCK_ROWS)
            if t < HALF:
                keep_ref[:, at] = r
            else:
                give_ref[:, at] = r.astype(jnp.bfloat16)
    for copy in picks:
        copy.wait()


def low_part(scalars, x, pieces):
    rows, width = x.shape
    hbm = pl.BlockSpec(memory_space=pl.ANY)
    return pl.pallas_call(
        low_kernel,
        grid_spec=pltpu.PrefetchScalarGridSpec(
            num_scalar_prefetch=1,
            grid=(1,),
            in_specs=[hbm] * 9,
            out_specs=[pl.BlockSpec((RANK, rows // 2), lambda i, s: (0, 0))] * 2 + [hbm],
            scratch_shapes=[
                pltpu.VMEM((rows, width), jnp.bfloat16),
                pltpu.VMEM((OWNERS * RANK, width), jnp.bfloat16),
                pltpu.SemaphoreType.DMA((8,)),
                pltpu.SemaphoreType.DMA((NBLK,)),
                pltpu.SemaphoreType.DMA((NBLK,)),
            ],
        ),
        out_shape=[
            jax.ShapeDtypeStruct((RANK, rows // 2), jnp.float32),
            jax.ShapeDtypeStruct((RANK, rows // 2), jnp.bfloat16),
            jax.ShapeDtypeStruct((NBLK * RANK, width), jnp.bfloat16),
        ],
        compiler_params=pltpu.CompilerParams(vmem_limit_bytes=VMEM_LIMIT),
        cost_estimate=SMALL,
        name="low_part",
    )(scalars, x, *pieces)


def up_kernel(s_ref, g_ref, mine_ref, other_ref, keep_ref, give_ref, gs, acc, sem_g):
    first = s_ref[PLACE + 1] * HALF
    width = acc.shape[1]
    columns = pl.ds(pl.multiple_of(s_ref[PLACE] * width, width), width)
    load = pltpu.make_async_copy(g_ref.at[:, columns], gs, sem_g)
    load.start()
    lane = lax.broadcasted_iota(jnp.int32, (RANK, BLOCK_ROWS), 1)
    acc[...] = jnp.zeros_like(acc)
    load.wait()
    for t in range(NBLK):
        b = lax.rem(first + t, NBLK)
        at = slice((t % HALF) * BLOCK_ROWS, (t % HALF + 1) * BLOCK_ROWS)
        low = (mine_ref if t < HALF else other_ref)[:, at]
        low = jnp.where(lane < s_ref[VALID + b], low.astype(jnp.float32), 0.0).astype(jnp.bfloat16)
        g = gs[pl.ds(pl.multiple_of(b * BLOCK_ROWS, BLOCK_ROWS), BLOCK_ROWS), :]
        r = ADAPTER_SCALE * jnp.dot(low, g, preferred_element_type=jnp.float32)
        slot = pl.ds(pl.multiple_of(s_ref[SLOT_OUT + b] * RANK, RANK), RANK)
        acc[slot, :] = r.astype(jnp.bfloat16)
    keep_ref[...] = acc[: NBLK * RANK, :]
    give_ref[...] = acc[NBLK * RANK :, :]


def up_part(scalars, cotangent, mine, other, width):
    rows = cotangent.shape[0]
    half = pl.BlockSpec(mine.shape, lambda i, s: (0, 0))
    out = jax.ShapeDtypeStruct((NBLK * RANK, width), jnp.bfloat16)
    return pl.pallas_call(
        up_kernel,
        grid_spec=pltpu.PrefetchScalarGridSpec(
            num_scalar_prefetch=1,
            grid=(1,),
            in_specs=[pl.BlockSpec(memory_space=pl.ANY), half, half],
            out_specs=[pl.BlockSpec((NBLK * RANK, width), lambda i, s: (0, 0))] * 2,
            scratch_shapes=[
                pltpu.VMEM((rows, width), jnp.bfloat16),
                pltpu.VMEM((OWNERS * RANK, width), jnp.bfloat16),
                pltpu.SemaphoreType.DMA,
            ],
        ),
        out_shape=[out, out],
        compiler_params=pltpu.CompilerParams(vmem_limit_bytes=VMEM_LIMIT),
        cost_estimate=SMALL,
        name="up_part",
    )(scalars, cotangent, mine, other)


def input_kernel(s_ref, g_ref, back_ref, picked_ref, *refs):
    v_pieces = refs[:8]
    out_ref, gs, staged, vs, maps, outs, sem_g, sem_v, sem_a, sem_o = refs[8:]
    features = vs.shape[0]
    share = features // OWNERS
    line = v_pieces[0].shape[0]
    loads_v = [
        pltpu.make_async_copy(p, staged.at[pl.ds(k * line, line), :], sem_v.at[k])
        for k, p in enumerate(v_pieces)
    ]
    load_a = pltpu.make_async_copy(picked_ref, maps, sem_a)
    step = 2 * BLOCK_ROWS
    loads_g, stores = [], []
    for t in range(HALF):
        at = pl.ds(t * step, step)
        to = pl.ds(t * step, step)
        loads_g.append(pltpu.make_async_copy(g_ref.at[at, :], gs.at[to, :], sem_g.at[t]))
        stores.append(pltpu.make_async_copy(outs.at[to, :], out_ref.at[at, :], sem_o.at[t]))
    for copy in loads_v + loads_g[:1] + [load_a] + loads_g[1:]:
        copy.start()
    for k in range(OWNERS):
        if k % SIDE == 0:
            loads_v[k // SIDE].wait()
        to = pl.ds(pl.multiple_of(s_ref[ORDER + k] * share, share), share)
        vs[to, :] = staged[k * share : (k + 1) * share, :]
    row = lax.broadcasted_iota(jnp.int32, (BLOCK_ROWS, features), 0)
    for t in range(HALF):
        loads_g[t].wait()
        if t == 0:
            load_a.wait()
        lives, terms = [], []
        for u in range(2):
            k = 2 * t + u
            g = gs[k * BLOCK_ROWS : (k + 1) * BLOCK_ROWS, :]
            lives.append(jnp.where(row < s_ref[VALID + k], g, jnp.zeros_like(g)))
            back = back_ref[:, k * BLOCK_ROWS : (k + 1) * BLOCK_ROWS]
            down = maps[k * RANK : (k + 1) * RANK, :]
            term = lax.dot_general(back, down, TN, preferred_element_type=jnp.float32)
            terms.append(term.astype(jnp.bfloat16).astype(jnp.float32))
        live = jnp.concatenate(lives, axis=0)
        frozen = jnp.dot(live, vs[...], preferred_element_type=jnp.float32)
        for u in range(2):
            k = 2 * t + u
            outs[k * BLOCK_ROWS : (k + 1) * BLOCK_ROWS, :] = (
                frozen[u * BLOCK_ROWS : (u + 1) * BLOCK_ROWS] + terms[u]
            ).astype(jnp.bfloat16)
        stores[t].start()
    for copy in stores:
        copy.wait()


def input_part(scalars, cotangent, back, picked, v_pieces):
    rows, features = cotangent.shape
    width = v_pieces[0].shape[1]
    hbm = pl.BlockSpec(memory_space=pl.ANY)
    half = pl.BlockSpec(back.shape, lambda i, s: (0, 0))
    return pl.pallas_call(
        input_kernel,
        grid_spec=pltpu.PrefetchScalarGridSpec(
            num_scalar_prefetch=1,
            grid=(1,),
            in_specs=[hbm, half] + [hbm] * 9,
            out_specs=hbm,
            scratch_shapes=[
                pltpu.VMEM((rows, features), jnp.bfloat16),
                pltpu.VMEM((features, width), jnp.bfloat16),
                pltpu.VMEM((features, width), jnp.bfloat16),
                pltpu.VMEM((NBLK * RANK, width), jnp.bfloat16),
                pltpu.VMEM((rows, width), jnp.bfloat16),
                pltpu.SemaphoreType.DMA((HALF,)),
                pltpu.SemaphoreType.DMA((8,)),
                pltpu.SemaphoreType.DMA,
                pltpu.SemaphoreType.DMA((HALF,)),
            ],
        ),
        out_shape=jax.ShapeDtypeStruct((rows, width), jnp.bfloat16),
        compiler_params=pltpu.CompilerParams(vmem_limit_bytes=VMEM_LIMIT),
        cost_estimate=SMALL,
        name="input_part",
    )(scalars, cotangent, back, picked, *v_pieces)


def make_scalars(task_of_block, valid_block_rows, adapter_of_task):
    w = lax.axis_index("wide")
    n = lax.axis_index("narrow")
    x, y, c = w // (2 * SIDE), (w // 2) % SIDE, w % 2
    hit = task_of_block == lax.broadcasted_iota(jnp.int32, (NBLK, OWNERS), 1)
    owner = jnp.sum(jnp.where(hit, adapter_of_task[None, :], 0), axis=1)
    ox, oy, oc = owner // (2 * SIDE), (owner // 2) % SIDE, owner % 2
    dx, dy = (x - ox) % SIDE, (y - oy) % SIDE
    i, j = jnp.where(oc == 0, dy, dx), jnp.where(oc == 0, dx, dy)
    side = (oc + c) % 2 * (SIDE * SIDE)
    slot_in = side + i * SIDE + j
    slot_out = side + (-i) % SIDE * SIDE + (-j) % SIDE
    k = lax.broadcasted_iota(jnp.int32, (OWNERS, 1), 0)[:, 0]
    kc = (k // (SIDE * SIDE) + c) % 2
    ki, kj = (k // SIDE) % SIDE, k % SIDE
    kx = (x - jnp.where(kc == 0, kj, ki)) % SIDE
    ky = (y - jnp.where(kc == 0, ki, kj)) % SIDE
    order = (kx * SIDE + ky) * 2 + kc
    spot = lax.broadcasted_iota(jnp.int32, (NBLK, 1), 0)[:, 0]
    place = jnp.where(spot == 0, n, n % 2)
    return jnp.concatenate([slot_in, slot_out, valid_block_rows, place, order])


def body(
    inputs,
    cotangent,
    value_matrix,
    adapter_down_maps,
    adapter_up_maps,
    task_of_block,
    valid_block_rows,
    adapter_of_task,
):
    scalars = make_scalars(task_of_block, valid_block_rows, adapter_of_task)
    up_own = adapter_up_maps[0]
    down_own = adapter_down_maps[0].T
    value_own = value_matrix.T

    got = gather_short(down_own)
    down_line = jnp.concatenate([down_own, got[1], got[2], got[3]], axis=0)
    own = jnp.concatenate([gather_narrow(up_own), value_own], axis=0)
    up_line, value_line = unpack(own, gather_short(own))
    down_pieces = gather_second(down_line)
    up_line, *down_pieces = tie(up_line, *down_pieces)

    up_pieces = gather_second(up_line)
    down_pieces = down_pieces + [swap_cores(p) for p in down_pieces]
    low_keep, low_give, picked = low_part(scalars, inputs, down_pieces)
    total = add_all(low_keep, [pair_step(low_give)])
    total, *up_pieces = tie(total, *up_pieces)

    up_pieces = up_pieces + [swap_cores(p) for p in up_pieces]
    total = exchange(total, 2)
    total, up_pieces = tie(total, up_pieces)

    back, down_keep, down_give = back_part(scalars, cotangent, inputs, up_pieces)
    low_mine = exchange(total, 4).astype(jnp.bfloat16)
    low_mine, down_keep, down_give, value_line = tie(low_mine, down_keep, down_give, value_line)

    down_got = swap_cores(down_give)
    low_other = pair_step(low_mine)
    value_pieces = gather_second(value_line)
    low_mine, low_other, down_keep, down_got, value_pieces = tie(
        low_mine, low_other, down_keep, down_got, value_pieces
    )

    up_keep, up_give = up_part(scalars, cotangent, low_mine, low_other, up_own.shape[1])
    lines = [
        jnp.concatenate(pair, axis=1)
        for pair in zip(
            merge_cores(down_keep, down_got), merge_cores(up_keep, swap_cores(up_give))
        )
    ]
    value_pieces = value_pieces + [swap_cores(p) for p in value_pieces]
    got = [shift(lines[d].astype(jnp.bfloat16), long_axis, d) for d in (1, 3, 2)]
    input_gradient = input_part(scalars, cotangent, back, picked, value_pieces)
    width = inputs.shape[1]
    line, input_gradient = tie(add_all(lines[0], got), input_gradient)

    down_grad, up_grad = reduce_short(line[:, :width], line[:, width:])
    return input_gradient, down_grad.T[None], up_grad[None]


def solution(mesh):
    return jax.shard_map(
        body,
        mesh=mesh,
        in_specs=(
            P("wide", "narrow"),
            P("wide", None),
            P("narrow", "wide"),
            P("wide", "narrow", None),
            P("wide", None, "narrow"),
            P("wide", None),
            P("wide"),
            P(),
        ),
        out_specs=(P("wide", "narrow"), P("wide", "narrow", None), P("wide", None, "narrow")),
        check_vma=False,
    )
```

```python
import jax
import jax.numpy as jnp
from jax import lax
from jax.experimental import pallas as pl
from jax.experimental.pallas import tpu as pltpu
from jax.sharding import PartitionSpec as P

BLOCK_ROWS = 128
ADAPTER_SCALE = 2.0
RANK = 64
SIDE = 4
NBLK = 16
OWNERS = 32
DEPTH = 8
HALF = NBLK // 2
VMEM_LIMIT = 48 * 1024 * 1024

SMALL = pl.CostEstimate(flops=1, bytes_accessed=1, transcendentals=0)

NT = (((1,), (1,)), ((), ()))
TN = (((0,), (0,)), ((), ()))

SLOT_IN, SLOT_OUT, VALID, PLACE, ORDER, SCALARS = 0, 16, 32, 48, 64, 96


def wide_index(x, y, c):
    return ((x % SIDE) * SIDE + (y % SIDE)) * 2 + c


def short_axis(d):
    return [
        (wide_index(x, y, c), wide_index(x + d, y, c) if c == 0 else wide_index(x, y + d, c))
        for x in range(SIDE)
        for y in range(SIDE)
        for c in range(2)
    ]


def long_axis(d):
    return [
        (wide_index(x, y, c), wide_index(x, y + d, c) if c == 0 else wide_index(x + d, y, c))
        for x in range(SIDE)
        for y in range(SIDE)
        for c in range(2)
    ]


def swap_cores(v):
    return lax.ppermute(v, "wide", [(w, w ^ 1) for w in range(OWNERS)])


def tie(*values):
    return lax.optimization_barrier(values)


def shift(v, axis, d):
    return lax.ppermute(v, "wide", axis(d))


def gather_short(own):
    return {d: shift(own, short_axis, d) for d in (1, 3, 2)}


def widen(own, other, q):
    late = (lax.axis_index("narrow") // q) % 2 == 1
    return jnp.concatenate([jnp.where(late, other, own), jnp.where(late, own, other)], axis=1)


def gather_second(line):
    got = {d: shift(line, long_axis, d) for d in (1, 3, 2)}
    return [line, got[1], got[2], got[3]]


def add_all(total, others):
    for other in others:
        total = total + other.astype(jnp.float32)
    return total


def send_line(down, up, axis, d):
    high = up.astype(jnp.bfloat16)
    rest = (up - high.astype(jnp.float32)).astype(jnp.bfloat16)
    got = shift(jnp.concatenate([down.astype(jnp.bfloat16), high, rest], axis=1), axis, d)
    width, share = down.shape[1], up.shape[1]
    got_up = got[:, width : width + share].astype(jnp.float32)
    return got[:, :width], got_up + got[:, width + share :].astype(jnp.float32)


def reduce_lines(downs, ups, axis):
    got = [send_line(downs[d], ups[d], axis, d) for d in (1, 3, 2)]
    return add_all(downs[0], [g[0] for g in got]), add_all(ups[0], [g[1] for g in got])


def split_rows(v):
    piece = v.shape[0] // SIDE
    return [v[i * piece : (i + 1) * piece] for i in range(SIDE)]


def narrow_send(v, f):
    return lax.ppermute(v, "narrow", [(i, f(i) % DEPTH) for i in range(DEPTH)])


def pair_step(v):
    return narrow_send(v, lambda i: i ^ 1)


def exchange(total, q):
    other = narrow_send(total.astype(jnp.bfloat16), lambda i: i ^ q)
    return total + other.astype(jnp.float32)


def block_at(b):
    return pl.ds(pl.multiple_of(b * BLOCK_ROWS, BLOCK_ROWS), BLOCK_ROWS)


def slot_at(slot):
    return pl.ds(pl.multiple_of(slot * RANK, RANK), RANK)


def back_kernel(s_ref, g_ref, x_ref, *refs):
    pieces, (back_ref, keep_ref, give_ref) = refs[:8], refs[8:11]
    gs, maps, xs, acc, sem_g, sem_b, sem_x, sem_o = refs[11:]
    per = pieces[0].shape[0]
    half_rows = NBLK * RANK
    loads = [
        pltpu.make_async_copy(p, maps.at[pl.ds(k * per, per), :], sem_b.at[k])
        for k, p in enumerate(pieces)
    ]
    g_loads, x_loads = [], []
    for t in range(HALF):
        at = pl.ds(2 * t * BLOCK_ROWS, 2 * BLOCK_ROWS)
        g_loads.append(pltpu.make_async_copy(g_ref.at[at, :], gs.at[at, :], sem_g.at[t]))
        x_loads.append(pltpu.make_async_copy(x_ref.at[at, :], xs.at[at, :], sem_x.at[t]))
    for copy in loads:
        copy.start()
    for t in range(HALF):
        g_loads[t].start()
        x_loads[t].start()
    acc[...] = jnp.zeros_like(acc)
    for copy in loads:
        copy.wait()
    lane = lax.broadcasted_iota(jnp.int32, (RANK, BLOCK_ROWS), 1)

    def backs(t):
        rows = slice(t * BLOCK_ROWS, (t + 2) * BLOCK_ROWS)
        ups = [maps[slot_at(s_ref[SLOT_IN + t + u]), :] for u in range(2)]
        pair = lax.dot_general(
            jnp.concatenate(ups, axis=0), gs[rows, :], NT, preferred_element_type=jnp.float32
        )
        parts = []
        for u in range(2):
            r = pair[u * RANK : (u + 1) * RANK, u * BLOCK_ROWS : (u + 1) * BLOCK_ROWS]
            r = jnp.where(lane < s_ref[VALID + t + u], ADAPTER_SCALE * r, 0.0)
            parts.append(r.astype(jnp.bfloat16))
        return parts

    def grads(t, parts):
        for u in range(2):
            b = t + u
            at = slice(b * BLOCK_ROWS, (b + 1) * BLOCK_ROWS)
            back_ref[:, at] = parts[u]
            grad = jnp.dot(parts[u], xs[at, :], preferred_element_type=jnp.float32)
            acc[slot_at(s_ref[SLOT_OUT + b]), :] = grad.astype(jnp.bfloat16)

    before = None
    for t in range(0, NBLK, 2):
        g_loads[t // 2].wait()
        if t:
            x_loads[t // 2 - 1].wait()
        parts = backs(t)
        if t:
            grads(t - 2, before)
        before = parts
    x_loads[HALF - 1].wait()
    grads(NBLK - 2, before)
    outs = [
        pltpu.make_async_copy(acc.at[pl.ds(half_rows, half_rows), :], give_ref, sem_o.at[0]),
        pltpu.make_async_copy(acc.at[pl.ds(0, half_rows), :], keep_ref, sem_o.at[1]),
    ]
    for copy in outs:
        copy.start()
    for copy in outs:
        copy.wait()


def back_part(scalars, cotangent, x, pieces):
    rows, features = cotangent.shape
    width = x.shape[1]
    hbm = pl.BlockSpec(memory_space=pl.ANY)
    out = jax.ShapeDtypeStruct((NBLK * RANK, width), jnp.bfloat16)
    return pl.pallas_call(
        back_kernel,
        grid_spec=pltpu.PrefetchScalarGridSpec(
            num_scalar_prefetch=1,
            grid=(1,),
            in_specs=[hbm] * 10,
            out_specs=[pl.BlockSpec((RANK, rows), lambda i, s: (0, 0)), hbm, hbm],
            scratch_shapes=[
                pltpu.VMEM((rows, features), jnp.bfloat16),
                pltpu.VMEM((OWNERS * RANK, features), jnp.bfloat16),
                pltpu.VMEM((rows, width), jnp.bfloat16),
                pltpu.VMEM((OWNERS * RANK, width), jnp.bfloat16),
                pltpu.SemaphoreType.DMA((HALF,)),
                pltpu.SemaphoreType.DMA((8,)),
                pltpu.SemaphoreType.DMA((HALF,)),
                pltpu.SemaphoreType.DMA((2,)),
            ],
        ),
        out_shape=[jax.ShapeDtypeStruct((RANK, rows), jnp.bfloat16), out, out],
        compiler_params=pltpu.CompilerParams(vmem_limit_bytes=VMEM_LIMIT),
        cost_estimate=pl.CostEstimate(
            flops=4 * rows * RANK * width, bytes_accessed=16 * 2**20, transcendentals=0
        ),
        name="back_part",
    )(scalars, cotangent, x, *pieces)


def low_kernel(s_ref, x_ref, *refs):
    pieces, (keep_ref, give_ref, picked_ref, xs, maps, sem_a, sem_x, sem_p) = refs[:8], refs[8:]
    per = pieces[0].shape[0]
    first = s_ref[PLACE + 1] * HALF
    loads = [
        pltpu.make_async_copy(p, maps.at[pl.ds(k * per, per), :], sem_a.at[k])
        for k, p in enumerate(pieces)
    ]
    blocks = []
    for t in range(NBLK):
        b = lax.rem(first + t, NBLK)
        at = pl.ds(pl.multiple_of(b * BLOCK_ROWS, BLOCK_ROWS), BLOCK_ROWS)
        to = pl.ds(t * BLOCK_ROWS, BLOCK_ROWS)
        blocks.append(pltpu.make_async_copy(x_ref.at[at, :], xs.at[to, :], sem_x.at[t]))
    for copy in loads + blocks:
        copy.start()
    for copy in loads:
        copy.wait()
    picks = []
    for b in range(NBLK):
        to = picked_ref.at[pl.ds(b * RANK, RANK), :]
        picks.append(
            pltpu.make_async_copy(maps.at[slot_at(s_ref[SLOT_IN + b]), :], to, sem_p.at[b])
        )
        picks[b].start()
    for t in range(0, NBLK, 2):
        if t % 4 == 0:
            for copy in blocks[t : t + 4]:
                copy.wait()
        downs = []
        for u in (t, t + 1):
            b = lax.rem(first + u, NBLK)
            downs.append(maps[slot_at(s_ref[SLOT_IN + b]), :])
        x = xs[t * BLOCK_ROWS : (t + 2) * BLOCK_ROWS, :]
        pair = lax.dot_general(
            jnp.concatenate(downs, axis=0), x, NT, preferred_element_type=jnp.float32
        )
        for u in range(2):
            r = pair[u * RANK : (u + 1) * RANK, u * BLOCK_ROWS : (u + 1) * BLOCK_ROWS]
            k = (t + u) % HALF
            at = slice(k * BLOCK_ROWS, (k + 1) * BLOCK_ROWS)
            if t < HALF:
                keep_ref[:, at] = r
            else:
                give_ref[:, at] = r.astype(jnp.bfloat16)
    for copy in picks:
        copy.wait()


def low_part(scalars, x, pieces):
    rows, width = x.shape
    hbm = pl.BlockSpec(memory_space=pl.ANY)
    return pl.pallas_call(
        low_kernel,
        grid_spec=pltpu.PrefetchScalarGridSpec(
            num_scalar_prefetch=1,
            grid=(1,),
            in_specs=[hbm] * 9,
            out_specs=[pl.BlockSpec((RANK, rows // 2), lambda i, s: (0, 0))] * 2 + [hbm],
            scratch_shapes=[
                pltpu.VMEM((rows, width), jnp.bfloat16),
                pltpu.VMEM((OWNERS * RANK, width), jnp.bfloat16),
                pltpu.SemaphoreType.DMA((8,)),
                pltpu.SemaphoreType.DMA((NBLK,)),
                pltpu.SemaphoreType.DMA((NBLK,)),
            ],
        ),
        out_shape=[
            jax.ShapeDtypeStruct((RANK, rows // 2), jnp.float32),
            jax.ShapeDtypeStruct((RANK, rows // 2), jnp.bfloat16),
            jax.ShapeDtypeStruct((NBLK * RANK, width), jnp.bfloat16),
        ],
        compiler_params=pltpu.CompilerParams(vmem_limit_bytes=VMEM_LIMIT),
        cost_estimate=SMALL,
        name="low_part",
    )(scalars, x, *pieces)


def up_kernel(s_ref, g_ref, mine_ref, other_ref, keep_ref, give_ref, gs, acc, sem_g):
    first = s_ref[PLACE + 1] * HALF
    width = acc.shape[1]
    columns = pl.ds(pl.multiple_of(s_ref[PLACE] * width, width), width)
    load = pltpu.make_async_copy(g_ref.at[:, columns], gs, sem_g)
    load.start()
    lane = lax.broadcasted_iota(jnp.int32, (RANK, BLOCK_ROWS), 1)
    acc[...] = jnp.zeros_like(acc)
    load.wait()
    for t in range(NBLK):
        b = lax.rem(first + t, NBLK)
        at = slice((t % HALF) * BLOCK_ROWS, (t % HALF + 1) * BLOCK_ROWS)
        low = (mine_ref if t < HALF else other_ref)[:, at]
        low = jnp.where(lane < s_ref[VALID + b], low.astype(jnp.float32), 0.0).astype(jnp.bfloat16)
        g = gs[pl.ds(pl.multiple_of(b * BLOCK_ROWS, BLOCK_ROWS), BLOCK_ROWS), :]
        r = ADAPTER_SCALE * jnp.dot(low, g, preferred_element_type=jnp.float32)
        acc[slot_at(s_ref[SLOT_OUT + b]), :] = r
    keep_ref[...] = acc[: NBLK * RANK, :]
    give_ref[...] = acc[NBLK * RANK :, :]


def up_part(scalars, cotangent, mine, other, width):
    rows = cotangent.shape[0]
    half = pl.BlockSpec(mine.shape, lambda i, s: (0, 0))
    out = jax.ShapeDtypeStruct((NBLK * RANK, width), jnp.float32)
    return pl.pallas_call(
        up_kernel,
        grid_spec=pltpu.PrefetchScalarGridSpec(
            num_scalar_prefetch=1,
            grid=(1,),
            in_specs=[pl.BlockSpec(memory_space=pl.ANY), half, half],
            out_specs=[pl.BlockSpec((NBLK * RANK, width), lambda i, s: (0, 0))] * 2,
            scratch_shapes=[
                pltpu.VMEM((rows, width), jnp.bfloat16),
                pltpu.VMEM((OWNERS * RANK, width), jnp.float32),
                pltpu.SemaphoreType.DMA,
            ],
        ),
        out_shape=[out, out],
        compiler_params=pltpu.CompilerParams(vmem_limit_bytes=VMEM_LIMIT),
        cost_estimate=SMALL,
        name="up_part",
    )(scalars, cotangent, mine, other)


def input_kernel(s_ref, g_ref, back_ref, picked_ref, *refs):
    v_pieces = refs[:8]
    out_ref, gs, staged, vs, maps, outs, sem_g, sem_v, sem_a, sem_o = refs[8:]
    features = vs.shape[0]
    share = features // OWNERS
    line = v_pieces[0].shape[0]
    loads_v = [
        pltpu.make_async_copy(p, staged.at[pl.ds(k * line, line), :], sem_v.at[k])
        for k, p in enumerate(v_pieces)
    ]
    load_a = pltpu.make_async_copy(picked_ref, maps, sem_a)
    step = 2 * BLOCK_ROWS
    loads_g, stores = [], []
    for t in range(HALF):
        at = pl.ds(t * step, step)
        to = pl.ds(t * step, step)
        loads_g.append(pltpu.make_async_copy(g_ref.at[at, :], gs.at[to, :], sem_g.at[t]))
        stores.append(pltpu.make_async_copy(outs.at[to, :], out_ref.at[at, :], sem_o.at[t]))
    for copy in loads_v + loads_g[:1] + [load_a] + loads_g[1:]:
        copy.start()
    for k in range(OWNERS):
        if k % SIDE == 0:
            loads_v[k // SIDE].wait()
        to = pl.ds(pl.multiple_of(s_ref[ORDER + k] * share, share), share)
        vs[to, :] = staged[k * share : (k + 1) * share, :]
    row = lax.broadcasted_iota(jnp.int32, (BLOCK_ROWS, features), 0)
    for t in range(HALF):
        loads_g[t].wait()
        if t == 0:
            load_a.wait()
        lives, terms = [], []
        for u in range(2):
            k = 2 * t + u
            g = gs[k * BLOCK_ROWS : (k + 1) * BLOCK_ROWS, :]
            lives.append(jnp.where(row < s_ref[VALID + k], g, jnp.zeros_like(g)))
            back = back_ref[:, k * BLOCK_ROWS : (k + 1) * BLOCK_ROWS]
            down = maps[k * RANK : (k + 1) * RANK, :]
            term = lax.dot_general(back, down, TN, preferred_element_type=jnp.float32)
            terms.append(term.astype(jnp.bfloat16).astype(jnp.float32))
        live = jnp.concatenate(lives, axis=0)
        frozen = jnp.dot(live, vs[...], preferred_element_type=jnp.float32)
        for u in range(2):
            k = 2 * t + u
            outs[k * BLOCK_ROWS : (k + 1) * BLOCK_ROWS, :] = (
                frozen[u * BLOCK_ROWS : (u + 1) * BLOCK_ROWS] + terms[u]
            ).astype(jnp.bfloat16)
        stores[t].start()
    for copy in stores:
        copy.wait()


def input_part(scalars, cotangent, back, picked, v_pieces):
    rows, features = cotangent.shape
    width = v_pieces[0].shape[1]
    hbm = pl.BlockSpec(memory_space=pl.ANY)
    half = pl.BlockSpec(back.shape, lambda i, s: (0, 0))
    return pl.pallas_call(
        input_kernel,
        grid_spec=pltpu.PrefetchScalarGridSpec(
            num_scalar_prefetch=1,
            grid=(1,),
            in_specs=[hbm, half] + [hbm] * 9,
            out_specs=hbm,
            scratch_shapes=[
                pltpu.VMEM((rows, features), jnp.bfloat16),
                pltpu.VMEM((features, width), jnp.bfloat16),
                pltpu.VMEM((features, width), jnp.bfloat16),
                pltpu.VMEM((NBLK * RANK, width), jnp.bfloat16),
                pltpu.VMEM((rows, width), jnp.bfloat16),
                pltpu.SemaphoreType.DMA((HALF,)),
                pltpu.SemaphoreType.DMA((8,)),
                pltpu.SemaphoreType.DMA,
                pltpu.SemaphoreType.DMA((HALF,)),
            ],
        ),
        out_shape=jax.ShapeDtypeStruct((rows, width), jnp.bfloat16),
        compiler_params=pltpu.CompilerParams(vmem_limit_bytes=VMEM_LIMIT),
        cost_estimate=SMALL,
        name="input_part",
    )(scalars, cotangent, back, picked, *v_pieces)


def make_scalars(task_of_block, valid_block_rows, adapter_of_task):
    w = lax.axis_index("wide")
    n = lax.axis_index("narrow")
    x, y, c = w // (2 * SIDE), (w // 2) % SIDE, w % 2
    hit = task_of_block == lax.broadcasted_iota(jnp.int32, (NBLK, OWNERS), 1)
    owner = jnp.sum(jnp.where(hit, adapter_of_task[None, :], 0), axis=1)
    ox, oy, oc = owner // (2 * SIDE), (owner // 2) % SIDE, owner % 2
    dx, dy = (x - ox) % SIDE, (y - oy) % SIDE
    i, j = jnp.where(oc == 0, dy, dx), jnp.where(oc == 0, dx, dy)
    side = (oc + c) % 2 * (SIDE * SIDE)
    slot_in = side + i * SIDE + j
    slot_out = side + (-i) % SIDE * SIDE + (-j) % SIDE
    k = lax.broadcasted_iota(jnp.int32, (OWNERS, 1), 0)[:, 0]
    kc = (k // (SIDE * SIDE) + c) % 2
    ki, kj = (k // SIDE) % SIDE, k % SIDE
    kx = (x - jnp.where(kc == 0, kj, ki)) % SIDE
    ky = (y - jnp.where(kc == 0, ki, kj)) % SIDE
    order = (kx * SIDE + ky) * 2 + kc
    spot = lax.broadcasted_iota(jnp.int32, (NBLK, 1), 0)[:, 0]
    place = jnp.where(spot == 0, n, n % 2)
    return jnp.concatenate([slot_in, slot_out, valid_block_rows, place, order])


def body(
    inputs,
    cotangent,
    value_matrix,
    adapter_down_maps,
    adapter_up_maps,
    task_of_block,
    valid_block_rows,
    adapter_of_task,
):
    scalars = make_scalars(task_of_block, valid_block_rows, adapter_of_task)
    up_own = adapter_up_maps[0]
    down_own = adapter_down_maps[0].T
    value_own = value_matrix.T

    got = gather_short(down_own)
    other = pair_step(up_own)
    other, got = tie(other, got)
    down_line = jnp.concatenate([down_own, got[1], got[2], got[3]], axis=0)
    down_pieces = gather_second(down_line)
    up_full = widen(up_own, other, 1)
    for q in (2, 4):
        up_full = widen(up_full, narrow_send(up_full, lambda i, q=q: i ^ q), q)
    own = jnp.concatenate([up_full, value_own], axis=0)
    own, *down_pieces = tie(own, *down_pieces)

    got = gather_short(own)
    parts = [own, got[1], got[2], got[3]]
    up_line = jnp.concatenate([p[:RANK] for p in parts], axis=0)
    down_pieces = down_pieces + [swap_cores(p) for p in down_pieces]
    low_keep, low_give, picked = low_part(scalars, inputs, down_pieces)
    total = add_all(low_keep, [pair_step(low_give)])
    total, up_line, parts = tie(total, up_line, parts)

    up_pieces = gather_second(up_line)
    low_mine = exchange(exchange(total, 2), 4).astype(jnp.bfloat16)
    low_mine, parts, *up_pieces = tie(low_mine, parts, *up_pieces)

    low_other = pair_step(low_mine)
    up_pieces = up_pieces + [swap_cores(p) for p in up_pieces]
    back, down_keep, down_give = back_part(scalars, cotangent, inputs, up_pieces)
    value_line = jnp.concatenate([p[RANK:] for p in parts], axis=0)
    low_mine, low_other, down_keep, down_give, value_line = tie(
        low_mine, low_other, down_keep, down_give, value_line
    )

    down_got = swap_cores(down_give)
    value_pieces = gather_second(value_line)
    up_keep, up_give = up_part(scalars, cotangent, low_mine, low_other, up_own.shape[1])
    up_keep, up_give, down_keep, down_got, value_pieces = tie(
        up_keep, up_give, down_keep, down_got, value_pieces
    )

    up_got = swap_cores(up_give)
    downs = [
        k.astype(jnp.float32) + g.astype(jnp.float32)
        for k, g in zip(split_rows(down_keep), split_rows(down_got))
    ]
    ups = [k + g for k, g in zip(split_rows(up_keep), split_rows(up_got))]
    value_pieces = value_pieces + [swap_cores(p) for p in value_pieces]
    down_line, up_line = reduce_lines(downs, ups, long_axis)
    input_gradient = input_part(scalars, cotangent, back, picked, value_pieces)
    down_line, up_line, input_gradient = tie(down_line, up_line, input_gradient)

    down_grad, up_grad = reduce_lines(split_rows(down_line), split_rows(up_line), short_axis)
    return input_gradient, down_grad.T[None], up_grad[None]


def solution(mesh):
    return jax.shard_map(
        body,
        mesh=mesh,
        in_specs=(
            P("wide", "narrow"),
            P("wide", None),
            P("narrow", "wide"),
            P("wide", "narrow", None),
            P("wide", None, "narrow"),
            P("wide", None),
            P("wide"),
            P(),
        ),
        out_specs=(P("wide", "narrow"), P("wide", "narrow", None), P("wide", None, "narrow")),
        check_vma=False,
    )
```

```python
import jax
import jax.numpy as jnp
from jax import lax
from jax.experimental import pallas as pl
from jax.experimental.pallas import tpu as pltpu
from jax.sharding import PartitionSpec as P

BLOCK_ROWS = 128
ADAPTER_SCALE = 2.0
RANK = 64
SIDE = 4
NBLK = 16
OWNERS = 32
DEPTH = 8
HALF = NBLK // 2
VMEM_LIMIT = 48 * 1024 * 1024

SMALL = pl.CostEstimate(flops=1, bytes_accessed=1, transcendentals=0)

NT = (((1,), (1,)), ((), ()))
TN = (((0,), (0,)), ((), ()))

SLOT_IN, SLOT_OUT, VALID, PLACE, ORDER, SCALARS = 0, 16, 32, 48, 64, 96


def wide_index(x, y, c):
    return ((x % SIDE) * SIDE + (y % SIDE)) * 2 + c


def short_axis(d):
    return [
        (wide_index(x, y, c), wide_index(x + d, y, c) if c == 0 else wide_index(x, y + d, c))
        for x in range(SIDE)
        for y in range(SIDE)
        for c in range(2)
    ]


def long_axis(d):
    return [
        (wide_index(x, y, c), wide_index(x, y + d, c) if c == 0 else wide_index(x + d, y, c))
        for x in range(SIDE)
        for y in range(SIDE)
        for c in range(2)
    ]


def swap_cores(v):
    return lax.ppermute(v, "wide", [(w, w ^ 1) for w in range(OWNERS)])


def tie(*values):
    return lax.optimization_barrier(values)


def shift(v, axis, d):
    return lax.ppermute(v, "wide", axis(d))


def gather_short(own):
    return {d: shift(own, short_axis, d) for d in (1, 3, 2)}


def widen(own, other, q):
    late = (lax.axis_index("narrow") // q) % 2 == 1
    return jnp.concatenate([jnp.where(late, other, own), jnp.where(late, own, other)], axis=1)


def gather_second(line):
    got = {d: shift(line, long_axis, d) for d in (1, 3, 2)}
    return [line, got[1], got[2], got[3]]


def add_all(total, others):
    for other in others:
        total = total + other.astype(jnp.float32)
    return total


def send_line(down, up, axis, d):
    high = up.astype(jnp.bfloat16)
    rest = (up - high.astype(jnp.float32)).astype(jnp.bfloat16)
    got = shift(jnp.concatenate([down.astype(jnp.bfloat16), high, rest], axis=1), axis, d)
    width, share = down.shape[1], up.shape[1]
    got_up = got[:, width : width + share].astype(jnp.float32)
    return got[:, :width], got_up + got[:, width + share :].astype(jnp.float32)


def reduce_lines(downs, ups, axis):
    got = [send_line(downs[d], ups[d], axis, d) for d in (1, 3, 2)]
    return add_all(downs[0], [g[0] for g in got]), add_all(ups[0], [g[1] for g in got])


def split_rows(v):
    piece = v.shape[0] // SIDE
    return [v[i * piece : (i + 1) * piece] for i in range(SIDE)]


def narrow_send(v, f):
    return lax.ppermute(v, "narrow", [(i, f(i) % DEPTH) for i in range(DEPTH)])


def pair_step(v):
    return narrow_send(v, lambda i: i ^ 1)


def exchange(total, q):
    other = narrow_send(total.astype(jnp.bfloat16), lambda i: i ^ q)
    return total + other.astype(jnp.float32)


def block_at(b):
    return pl.ds(pl.multiple_of(b * BLOCK_ROWS, BLOCK_ROWS), BLOCK_ROWS)


def slot_at(slot):
    return pl.ds(pl.multiple_of(slot * RANK, RANK), RANK)


def back_kernel(s_ref, g_ref, x_ref, *refs):
    pieces, (back_ref, keep_ref, give_ref) = refs[:8], refs[8:11]
    gs, maps, xs, acc, sem_g, sem_b, sem_x, sem_o = refs[11:]
    per = pieces[0].shape[0]
    half_rows = NBLK * RANK
    loads = [
        pltpu.make_async_copy(p, maps.at[pl.ds(k * per, per), :], sem_b.at[k])
        for k, p in enumerate(pieces)
    ]
    g_loads, x_loads = [], []
    for t in range(HALF):
        at = pl.ds(2 * t * BLOCK_ROWS, 2 * BLOCK_ROWS)
        g_loads.append(pltpu.make_async_copy(g_ref.at[at, :], gs.at[at, :], sem_g.at[t]))
        x_loads.append(pltpu.make_async_copy(x_ref.at[at, :], xs.at[at, :], sem_x.at[t]))
    for copy in loads:
        copy.start()
    for t in range(HALF):
        g_loads[t].start()
        x_loads[t].start()
    acc[...] = jnp.zeros_like(acc)
    for copy in loads:
        copy.wait()
    lane = lax.broadcasted_iota(jnp.int32, (RANK, BLOCK_ROWS), 1)

    def backs(t):
        rows = slice(t * BLOCK_ROWS, (t + 2) * BLOCK_ROWS)
        ups = [maps[slot_at(s_ref[SLOT_IN + t + u]), :] for u in range(2)]
        pair = lax.dot_general(
            jnp.concatenate(ups, axis=0), gs[rows, :], NT, preferred_element_type=jnp.float32
        )
        parts = []
        for u in range(2):
            r = pair[u * RANK : (u + 1) * RANK, u * BLOCK_ROWS : (u + 1) * BLOCK_ROWS]
            r = jnp.where(lane < s_ref[VALID + t + u], ADAPTER_SCALE * r, 0.0)
            parts.append(r.astype(jnp.bfloat16))
        return parts

    def grads(t, parts):
        for u in range(2):
            b = t + u
            at = slice(b * BLOCK_ROWS, (b + 1) * BLOCK_ROWS)
            back_ref[:, at] = parts[u]
            grad = jnp.dot(parts[u], xs[at, :], preferred_element_type=jnp.float32)
            acc[slot_at(s_ref[SLOT_OUT + b]), :] = grad.astype(jnp.bfloat16)

    before = None
    for t in range(0, NBLK, 2):
        g_loads[t // 2].wait()
        if t:
            x_loads[t // 2 - 1].wait()
        parts = backs(t)
        if t:
            grads(t - 2, before)
        before = parts
    x_loads[HALF - 1].wait()
    grads(NBLK - 2, before)
    outs = [
        pltpu.make_async_copy(acc.at[pl.ds(half_rows, half_rows), :], give_ref, sem_o.at[0]),
        pltpu.make_async_copy(acc.at[pl.ds(0, half_rows), :], keep_ref, sem_o.at[1]),
    ]
    for copy in outs:
        copy.start()
    for copy in outs:
        copy.wait()


def back_part(scalars, cotangent, x, pieces):
    rows, features = cotangent.shape
    width = x.shape[1]
    hbm = pl.BlockSpec(memory_space=pl.ANY)
    out = jax.ShapeDtypeStruct((NBLK * RANK, width), jnp.bfloat16)
    return pl.pallas_call(
        back_kernel,
        grid_spec=pltpu.PrefetchScalarGridSpec(
            num_scalar_prefetch=1,
            grid=(1,),
            in_specs=[hbm] * 10,
            out_specs=[pl.BlockSpec((RANK, rows), lambda i, s: (0, 0)), hbm, hbm],
            scratch_shapes=[
                pltpu.VMEM((rows, features), jnp.bfloat16),
                pltpu.VMEM((OWNERS * RANK, features), jnp.bfloat16),
                pltpu.VMEM((rows, width), jnp.bfloat16),
                pltpu.VMEM((OWNERS * RANK, width), jnp.bfloat16),
                pltpu.SemaphoreType.DMA((HALF,)),
                pltpu.SemaphoreType.DMA((8,)),
                pltpu.SemaphoreType.DMA((HALF,)),
                pltpu.SemaphoreType.DMA((2,)),
            ],
        ),
        out_shape=[jax.ShapeDtypeStruct((RANK, rows), jnp.bfloat16), out, out],
        compiler_params=pltpu.CompilerParams(vmem_limit_bytes=VMEM_LIMIT),
        cost_estimate=pl.CostEstimate(
            flops=4 * rows * RANK * width, bytes_accessed=16 * 2**20, transcendentals=0
        ),
        name="back_part",
    )(scalars, cotangent, x, *pieces)


def low_kernel(s_ref, x_ref, *refs):
    pieces, (keep_ref, give_ref, picked_ref, xs, maps, sem_a, sem_x, sem_p) = refs[:8], refs[8:]
    per = pieces[0].shape[0]
    first = s_ref[PLACE + 1] * HALF
    loads = [
        pltpu.make_async_copy(p, maps.at[pl.ds(k * per, per), :], sem_a.at[k])
        for k, p in enumerate(pieces)
    ]
    blocks = []
    for t in range(NBLK):
        b = lax.rem(first + t, NBLK)
        at = pl.ds(pl.multiple_of(b * BLOCK_ROWS, BLOCK_ROWS), BLOCK_ROWS)
        to = pl.ds(t * BLOCK_ROWS, BLOCK_ROWS)
        blocks.append(pltpu.make_async_copy(x_ref.at[at, :], xs.at[to, :], sem_x.at[t]))
    for copy in loads + blocks:
        copy.start()
    for copy in loads:
        copy.wait()
    picks = []
    for b in range(NBLK):
        to = picked_ref.at[pl.ds(b * RANK, RANK), :]
        picks.append(
            pltpu.make_async_copy(maps.at[slot_at(s_ref[SLOT_IN + b]), :], to, sem_p.at[b])
        )
        picks[b].start()
    for t in range(0, NBLK, 2):
        if t % 4 == 0:
            for copy in blocks[t : t + 4]:
                copy.wait()
        downs = []
        for u in (t, t + 1):
            b = lax.rem(first + u, NBLK)
            downs.append(maps[slot_at(s_ref[SLOT_IN + b]), :])
        x = xs[t * BLOCK_ROWS : (t + 2) * BLOCK_ROWS, :]
        pair = lax.dot_general(
            jnp.concatenate(downs, axis=0), x, NT, preferred_element_type=jnp.float32
        )
        for u in range(2):
            r = pair[u * RANK : (u + 1) * RANK, u * BLOCK_ROWS : (u + 1) * BLOCK_ROWS]
            k = (t + u) % HALF
            at = slice(k * BLOCK_ROWS, (k + 1) * BLOCK_ROWS)
            if t < HALF:
                keep_ref[:, at] = r
            else:
                give_ref[:, at] = r.astype(jnp.bfloat16)
    for copy in picks:
        copy.wait()


def low_part(scalars, x, pieces):
    rows, width = x.shape
    hbm = pl.BlockSpec(memory_space=pl.ANY)
    return pl.pallas_call(
        low_kernel,
        grid_spec=pltpu.PrefetchScalarGridSpec(
            num_scalar_prefetch=1,
            grid=(1,),
            in_specs=[hbm] * 9,
            out_specs=[pl.BlockSpec((RANK, rows // 2), lambda i, s: (0, 0))] * 2 + [hbm],
            scratch_shapes=[
                pltpu.VMEM((rows, width), jnp.bfloat16),
                pltpu.VMEM((OWNERS * RANK, width), jnp.bfloat16),
                pltpu.SemaphoreType.DMA((8,)),
                pltpu.SemaphoreType.DMA((NBLK,)),
                pltpu.SemaphoreType.DMA((NBLK,)),
            ],
        ),
        out_shape=[
            jax.ShapeDtypeStruct((RANK, rows // 2), jnp.float32),
            jax.ShapeDtypeStruct((RANK, rows // 2), jnp.bfloat16),
            jax.ShapeDtypeStruct((NBLK * RANK, width), jnp.bfloat16),
        ],
        compiler_params=pltpu.CompilerParams(vmem_limit_bytes=VMEM_LIMIT),
        cost_estimate=SMALL,
        name="low_part",
    )(scalars, x, *pieces)


def up_kernel(s_ref, g_ref, mine_ref, other_ref, keep_ref, give_ref, gs, acc, sem_g):
    first = s_ref[PLACE + 1] * HALF
    width = acc.shape[1]
    columns = pl.ds(pl.multiple_of(s_ref[PLACE] * width, width), width)
    load = pltpu.make_async_copy(g_ref.at[:, columns], gs, sem_g)
    load.start()
    lane = lax.broadcasted_iota(jnp.int32, (RANK, BLOCK_ROWS), 1)
    acc[...] = jnp.zeros_like(acc)
    load.wait()
    for t in range(NBLK):
        b = lax.rem(first + t, NBLK)
        at = slice((t % HALF) * BLOCK_ROWS, (t % HALF + 1) * BLOCK_ROWS)
        low = (mine_ref if t < HALF else other_ref)[:, at]
        low = jnp.where(lane < s_ref[VALID + b], low.astype(jnp.float32), 0.0).astype(jnp.bfloat16)
        g = gs[pl.ds(pl.multiple_of(b * BLOCK_ROWS, BLOCK_ROWS), BLOCK_ROWS), :]
        r = ADAPTER_SCALE * jnp.dot(low, g, preferred_element_type=jnp.float32)
        acc[slot_at(s_ref[SLOT_OUT + b]), :] = r
    keep_ref[...] = acc[: NBLK * RANK, :]
    give_ref[...] = acc[NBLK * RANK :, :]


def up_part(scalars, cotangent, mine, other, width):
    rows = cotangent.shape[0]
    half = pl.BlockSpec(mine.shape, lambda i, s: (0, 0))
    out = jax.ShapeDtypeStruct((NBLK * RANK, width), jnp.float32)
    return pl.pallas_call(
        up_kernel,
        grid_spec=pltpu.PrefetchScalarGridSpec(
            num_scalar_prefetch=1,
            grid=(1,),
            in_specs=[pl.BlockSpec(memory_space=pl.ANY), half, half],
            out_specs=[pl.BlockSpec((NBLK * RANK, width), lambda i, s: (0, 0))] * 2,
            scratch_shapes=[
                pltpu.VMEM((rows, width), jnp.bfloat16),
                pltpu.VMEM((OWNERS * RANK, width), jnp.float32),
                pltpu.SemaphoreType.DMA,
            ],
        ),
        out_shape=[out, out],
        compiler_params=pltpu.CompilerParams(vmem_limit_bytes=VMEM_LIMIT),
        cost_estimate=SMALL,
        name="up_part",
    )(scalars, cotangent, mine, other)


def input_kernel(s_ref, g_ref, back_ref, picked_ref, *refs):
    v_pieces = refs[:8]
    out_ref, gs, staged, vs, maps, outs, sem_g, sem_v, sem_a, sem_o = refs[8:]
    features = vs.shape[0]
    share = features // OWNERS
    line = v_pieces[0].shape[0]
    loads_v = [
        pltpu.make_async_copy(p, staged.at[pl.ds(k * line, line), :], sem_v.at[k])
        for k, p in enumerate(v_pieces)
    ]
    load_a = pltpu.make_async_copy(picked_ref, maps, sem_a)
    step = 2 * BLOCK_ROWS
    loads_g, stores = [], []
    for t in range(HALF):
        at = pl.ds(t * step, step)
        to = pl.ds(t * step, step)
        loads_g.append(pltpu.make_async_copy(g_ref.at[at, :], gs.at[to, :], sem_g.at[t]))
        stores.append(pltpu.make_async_copy(outs.at[to, :], out_ref.at[at, :], sem_o.at[t]))
    for copy in loads_v + loads_g[:1] + [load_a] + loads_g[1:]:
        copy.start()
    for k in range(OWNERS):
        if k % SIDE == 0:
            loads_v[k // SIDE].wait()
        to = pl.ds(pl.multiple_of(s_ref[ORDER + k] * share, share), share)
        vs[to, :] = staged[k * share : (k + 1) * share, :]
    row = lax.broadcasted_iota(jnp.int32, (BLOCK_ROWS, features), 0)
    for t in range(HALF):
        loads_g[t].wait()
        if t == 0:
            load_a.wait()
        lives, terms = [], []
        for u in range(2):
            k = 2 * t + u
            g = gs[k * BLOCK_ROWS : (k + 1) * BLOCK_ROWS, :]
            lives.append(jnp.where(row < s_ref[VALID + k], g, jnp.zeros_like(g)))
            back = back_ref[:, k * BLOCK_ROWS : (k + 1) * BLOCK_ROWS]
            down = maps[k * RANK : (k + 1) * RANK, :]
            term = lax.dot_general(back, down, TN, preferred_element_type=jnp.float32)
            terms.append(term.astype(jnp.bfloat16).astype(jnp.float32))
        live = jnp.concatenate(lives, axis=0)
        frozen = jnp.dot(live, vs[...], preferred_element_type=jnp.float32)
        for u in range(2):
            k = 2 * t + u
            outs[k * BLOCK_ROWS : (k + 1) * BLOCK_ROWS, :] = (
                frozen[u * BLOCK_ROWS : (u + 1) * BLOCK_ROWS] + terms[u]
            ).astype(jnp.bfloat16)
        stores[t].start()
    for copy in stores:
        copy.wait()


def input_part(scalars, cotangent, back, picked, v_pieces):
    rows, features = cotangent.shape
    width = v_pieces[0].shape[1]
    hbm = pl.BlockSpec(memory_space=pl.ANY)
    half = pl.BlockSpec(back.shape, lambda i, s: (0, 0))
    return pl.pallas_call(
        input_kernel,
        grid_spec=pltpu.PrefetchScalarGridSpec(
            num_scalar_prefetch=1,
            grid=(1,),
            in_specs=[hbm, half] + [hbm] * 9,
            out_specs=hbm,
            scratch_shapes=[
                pltpu.VMEM((rows, features), jnp.bfloat16),
                pltpu.VMEM((features, width), jnp.bfloat16),
                pltpu.VMEM((features, width), jnp.bfloat16),
                pltpu.VMEM((NBLK * RANK, width), jnp.bfloat16),
                pltpu.VMEM((rows, width), jnp.bfloat16),
                pltpu.SemaphoreType.DMA((HALF,)),
                pltpu.SemaphoreType.DMA((8,)),
                pltpu.SemaphoreType.DMA,
                pltpu.SemaphoreType.DMA((HALF,)),
            ],
        ),
        out_shape=jax.ShapeDtypeStruct((rows, width), jnp.bfloat16),
        compiler_params=pltpu.CompilerParams(vmem_limit_bytes=VMEM_LIMIT),
        cost_estimate=SMALL,
        name="input_part",
    )(scalars, cotangent, back, picked, *v_pieces)


def make_scalars(task_of_block, valid_block_rows, adapter_of_task):
    w = lax.axis_index("wide")
    n = lax.axis_index("narrow")
    x, y, c = w // (2 * SIDE), (w // 2) % SIDE, w % 2
    hit = task_of_block == lax.broadcasted_iota(jnp.int32, (NBLK, OWNERS), 1)
    owner = jnp.sum(jnp.where(hit, adapter_of_task[None, :], 0), axis=1)
    ox, oy, oc = owner // (2 * SIDE), (owner // 2) % SIDE, owner % 2
    dx, dy = (x - ox) % SIDE, (y - oy) % SIDE
    i, j = jnp.where(oc == 0, dy, dx), jnp.where(oc == 0, dx, dy)
    side = (oc + c) % 2 * (SIDE * SIDE)
    slot_in = side + i * SIDE + j
    slot_out = side + (-i) % SIDE * SIDE + (-j) % SIDE
    k = lax.broadcasted_iota(jnp.int32, (OWNERS, 1), 0)[:, 0]
    kc = (k // (SIDE * SIDE) + c) % 2
    ki, kj = (k // SIDE) % SIDE, k % SIDE
    kx = (x - jnp.where(kc == 0, kj, ki)) % SIDE
    ky = (y - jnp.where(kc == 0, ki, kj)) % SIDE
    order = (kx * SIDE + ky) * 2 + kc
    spot = lax.broadcasted_iota(jnp.int32, (NBLK, 1), 0)[:, 0]
    place = jnp.where(spot == 0, n, n % 2)
    return jnp.concatenate([slot_in, slot_out, valid_block_rows, place, order])


def body(
    inputs,
    cotangent,
    value_matrix,
    adapter_down_maps,
    adapter_up_maps,
    task_of_block,
    valid_block_rows,
    adapter_of_task,
):
    scalars = make_scalars(task_of_block, valid_block_rows, adapter_of_task)
    up_own = adapter_up_maps[0]
    down_own = adapter_down_maps[0].T
    value_own = value_matrix.T

    got = gather_short(down_own)
    other = pair_step(up_own)
    up_full = widen(up_own, other, 1)
    up_full = widen(up_full, narrow_send(up_full, lambda i: i ^ 2), 2)
    up_full, got, scalars = tie(up_full, got, scalars)

    down_line = jnp.concatenate([down_own, got[1], got[2], got[3]], axis=0)
    down_pieces = gather_second(down_line)
    up_full = widen(up_full, narrow_send(up_full, lambda i: i ^ 4), 4)
    own = jnp.concatenate([up_full, value_own], axis=0)
    got = gather_short(own)
    parts = [own, got[1], got[2], got[3]]
    up_line = jnp.concatenate([p[:RANK] for p in parts], axis=0)
    up_line, parts, *down_pieces = tie(up_line, parts, *down_pieces)

    up_pieces = gather_second(up_line)
    up_first = swap_cores(up_line)
    down_pieces = down_pieces + [swap_cores(p) for p in down_pieces]
    low_keep, low_give, picked = low_part(scalars, inputs, down_pieces)
    total = add_all(low_keep, [pair_step(low_give)])
    total, parts, up_first, *up_pieces = tie(total, parts, up_first, *up_pieces)

    up_pieces = up_pieces + [up_first] + [swap_cores(p) for p in up_pieces[1:]]
    total = exchange(total, 2)
    value_line = jnp.concatenate([p[RANK:] for p in parts], axis=0)
    total, value_line, *up_pieces = tie(total, value_line, *up_pieces)

    value_pieces = gather_second(value_line)
    low_mine = exchange(total, 4).astype(jnp.bfloat16)
    back, down_keep, down_give = back_part(scalars, cotangent, inputs, up_pieces)
    low_mine, down_keep, down_give, value_pieces = tie(
        low_mine, down_keep, down_give, value_pieces
    )

    down_got = swap_cores(down_give)
    low_other = pair_step(low_mine)
    up_keep, up_give = up_part(scalars, cotangent, low_mine, low_other, up_own.shape[1])
    up_got = swap_cores(up_give)
    value_pieces = value_pieces + [swap_cores(p) for p in value_pieces]
    up_keep, up_got, down_keep, down_got, value_pieces = tie(
        up_keep, up_got, down_keep, down_got, value_pieces
    )

    downs = [
        k.astype(jnp.float32) + g.astype(jnp.float32)
        for k, g in zip(split_rows(down_keep), split_rows(down_got))
    ]
    ups = [k + g for k, g in zip(split_rows(up_keep), split_rows(up_got))]
    down_line, up_line = reduce_lines(downs, ups, long_axis)
    input_gradient = input_part(scalars, cotangent, back, picked, value_pieces)
    down_line, up_line, input_gradient = tie(down_line, up_line, input_gradient)

    down_grad, up_grad = reduce_lines(split_rows(down_line), split_rows(up_line), short_axis)
    return input_gradient, down_grad.T[None], up_grad[None]


def solution(mesh):
    return jax.shard_map(
        body,
        mesh=mesh,
        in_specs=(
            P("wide", "narrow"),
            P("wide", None),
            P("narrow", "wide"),
            P("wide", "narrow", None),
            P("wide", None, "narrow"),
            P("wide", None),
            P("wide"),
            P(),
        ),
        out_specs=(P("wide", "narrow"), P("wide", "narrow", None), P("wide", None, "narrow")),
        check_vma=False,
    )
```

```python
import jax
import jax.numpy as jnp
from jax import lax
from jax.experimental import pallas as pl
from jax.experimental.pallas import tpu as pltpu
from jax.sharding import PartitionSpec as P

BLOCK_ROWS = 128
ADAPTER_SCALE = 2.0
RANK = 64
SIDE = 4
NBLK = 16
OWNERS = 32
DEPTH = 8
HALF = NBLK // 2
VMEM_LIMIT = 48 * 1024 * 1024

SMALL = pl.CostEstimate(flops=1, bytes_accessed=1, transcendentals=0)

NT = (((1,), (1,)), ((), ()))
TN = (((0,), (0,)), ((), ()))

SLOT_IN, SLOT_OUT, VALID, PLACE, ORDER, SCALARS = 0, 16, 32, 48, 64, 96


def wide_index(x, y, c):
    return ((x % SIDE) * SIDE + (y % SIDE)) * 2 + c


def short_axis(d):
    return [
        (wide_index(x, y, c), wide_index(x + d, y, c) if c == 0 else wide_index(x, y + d, c))
        for x in range(SIDE)
        for y in range(SIDE)
        for c in range(2)
    ]


def long_axis(d):
    return [
        (wide_index(x, y, c), wide_index(x, y + d, c) if c == 0 else wide_index(x + d, y, c))
        for x in range(SIDE)
        for y in range(SIDE)
        for c in range(2)
    ]


def swap_cores(v):
    return lax.ppermute(v, "wide", [(w, w ^ 1) for w in range(OWNERS)])


def tie(*values):
    return lax.optimization_barrier(values)


def shift(v, axis, d):
    return lax.ppermute(v, "wide", axis(d))


def gather_short(own):
    return {d: shift(own, short_axis, d) for d in (1, 3, 2)}


def widen(own, other, q):
    late = (lax.axis_index("narrow") // q) % 2 == 1
    return jnp.concatenate([jnp.where(late, other, own), jnp.where(late, own, other)], axis=1)


def gather_second(line):
    got = {d: shift(line, long_axis, d) for d in (1, 3, 2)}
    return [line, got[1], got[2], got[3]]


def add_all(total, others):
    for other in others:
        total = total + other.astype(jnp.float32)
    return total


def send_line(down, up, axis, d):
    high = up.astype(jnp.bfloat16)
    rest = (up - high.astype(jnp.float32)).astype(jnp.bfloat16)
    got = shift(jnp.concatenate([down.astype(jnp.bfloat16), high, rest], axis=1), axis, d)
    width, share = down.shape[1], up.shape[1]
    got_up = got[:, width : width + share].astype(jnp.float32)
    return got[:, :width], got_up + got[:, width + share :].astype(jnp.float32)


def reduce_lines(downs, ups, axis):
    got = [send_line(downs[d], ups[d], axis, d) for d in (1, 3, 2)]
    return add_all(downs[0], [g[0] for g in got]), add_all(ups[0], [g[1] for g in got])


def split_rows(v):
    piece = v.shape[0] // SIDE
    return [v[i * piece : (i + 1) * piece] for i in range(SIDE)]


def narrow_send(v, f):
    return lax.ppermute(v, "narrow", [(i, f(i) % DEPTH) for i in range(DEPTH)])


def pair_step(v):
    return narrow_send(v, lambda i: i ^ 1)


def exchange(total, q):
    other = narrow_send(total.astype(jnp.bfloat16), lambda i: i ^ q)
    return total + other.astype(jnp.float32)


def block_at(b):
    return pl.ds(pl.multiple_of(b * BLOCK_ROWS, BLOCK_ROWS), BLOCK_ROWS)


def slot_at(slot):
    return pl.ds(pl.multiple_of(slot * RANK, RANK), RANK)


def back_kernel(s_ref, g_ref, x_ref, *refs):
    pieces, (back_ref, keep_ref, give_ref) = refs[:8], refs[8:11]
    gs, maps, xs, acc, sem_g, sem_b, sem_x, sem_o = refs[11:]
    per = pieces[0].shape[0]
    half_rows = NBLK * RANK
    loads = [
        pltpu.make_async_copy(p, maps.at[pl.ds(k * per, per), :], sem_b.at[k])
        for k, p in enumerate(pieces)
    ]
    g_loads, x_loads = [], []
    for t in range(HALF):
        at = pl.ds(2 * t * BLOCK_ROWS, 2 * BLOCK_ROWS)
        g_loads.append(pltpu.make_async_copy(g_ref.at[at, :], gs.at[at, :], sem_g.at[t]))
        x_loads.append(pltpu.make_async_copy(x_ref.at[at, :], xs.at[at, :], sem_x.at[t]))
    for copy in loads:
        copy.start()
    for t in range(HALF):
        g_loads[t].start()
        x_loads[t].start()
    acc[...] = jnp.zeros_like(acc)
    for copy in loads:
        copy.wait()
    lane = lax.broadcasted_iota(jnp.int32, (RANK, BLOCK_ROWS), 1)

    def backs(t):
        rows = slice(t * BLOCK_ROWS, (t + 2) * BLOCK_ROWS)
        ups = [maps[slot_at(s_ref[SLOT_IN + t + u]), :] for u in range(2)]
        pair = lax.dot_general(
            jnp.concatenate(ups, axis=0), gs[rows, :], NT, preferred_element_type=jnp.float32
        )
        parts = []
        for u in range(2):
            r = pair[u * RANK : (u + 1) * RANK, u * BLOCK_ROWS : (u + 1) * BLOCK_ROWS]
            r = jnp.where(lane < s_ref[VALID + t + u], ADAPTER_SCALE * r, 0.0)
            parts.append(r.astype(jnp.bfloat16))
        return parts

    def grads(t, parts):
        for u in range(2):
            b = t + u
            at = slice(b * BLOCK_ROWS, (b + 1) * BLOCK_ROWS)
            back_ref[:, at] = parts[u]
            grad = jnp.dot(parts[u], xs[at, :], preferred_element_type=jnp.float32)
            acc[slot_at(s_ref[SLOT_OUT + b]), :] = grad.astype(jnp.bfloat16)

    before = None
    for t in range(0, NBLK, 2):
        g_loads[t // 2].wait()
        if t:
            x_loads[t // 2 - 1].wait()
        parts = backs(t)
        if t:
            grads(t - 2, before)
        before = parts
    x_loads[HALF - 1].wait()
    grads(NBLK - 2, before)
    outs = [
        pltpu.make_async_copy(acc.at[pl.ds(half_rows, half_rows), :], give_ref, sem_o.at[0]),
        pltpu.make_async_copy(acc.at[pl.ds(0, half_rows), :], keep_ref, sem_o.at[1]),
    ]
    for copy in outs:
        copy.start()
    for copy in outs:
        copy.wait()


def back_part(scalars, cotangent, x, pieces):
    rows, features = cotangent.shape
    width = x.shape[1]
    hbm = pl.BlockSpec(memory_space=pl.ANY)
    out = jax.ShapeDtypeStruct((NBLK * RANK, width), jnp.bfloat16)
    return pl.pallas_call(
        back_kernel,
        grid_spec=pltpu.PrefetchScalarGridSpec(
            num_scalar_prefetch=1,
            grid=(1,),
            in_specs=[hbm] * 10,
            out_specs=[pl.BlockSpec((RANK, rows), lambda i, s: (0, 0)), hbm, hbm],
            scratch_shapes=[
                pltpu.VMEM((rows, features), jnp.bfloat16),
                pltpu.VMEM((OWNERS * RANK, features), jnp.bfloat16),
                pltpu.VMEM((rows, width), jnp.bfloat16),
                pltpu.VMEM((OWNERS * RANK, width), jnp.bfloat16),
                pltpu.SemaphoreType.DMA((HALF,)),
                pltpu.SemaphoreType.DMA((8,)),
                pltpu.SemaphoreType.DMA((HALF,)),
                pltpu.SemaphoreType.DMA((2,)),
            ],
        ),
        out_shape=[jax.ShapeDtypeStruct((RANK, rows), jnp.bfloat16), out, out],
        compiler_params=pltpu.CompilerParams(vmem_limit_bytes=VMEM_LIMIT),
        cost_estimate=pl.CostEstimate(
            flops=4 * rows * RANK * width, bytes_accessed=16 * 2**20, transcendentals=0
        ),
        name="back_part",
    )(scalars, cotangent, x, *pieces)


def low_kernel(s_ref, x_ref, *refs):
    pieces, (keep_ref, give_ref, picked_ref, xs, maps, sem_a, sem_x, sem_p) = refs[:8], refs[8:]
    per = pieces[0].shape[0]
    first = s_ref[PLACE + 1] * HALF
    loads = [
        pltpu.make_async_copy(p, maps.at[pl.ds(k * per, per), :], sem_a.at[k])
        for k, p in enumerate(pieces)
    ]
    blocks = []
    for t in range(NBLK):
        b = lax.rem(first + t, NBLK)
        at = pl.ds(pl.multiple_of(b * BLOCK_ROWS, BLOCK_ROWS), BLOCK_ROWS)
        to = pl.ds(t * BLOCK_ROWS, BLOCK_ROWS)
        blocks.append(pltpu.make_async_copy(x_ref.at[at, :], xs.at[to, :], sem_x.at[t]))
    for copy in loads + blocks:
        copy.start()
    for copy in loads:
        copy.wait()
    picks = []
    for b in range(NBLK):
        to = picked_ref.at[pl.ds(b * RANK, RANK), :]
        picks.append(
            pltpu.make_async_copy(maps.at[slot_at(s_ref[SLOT_IN + b]), :], to, sem_p.at[b])
        )
        picks[b].start()
    for t in range(0, NBLK, 2):
        if t % 4 == 0:
            for copy in blocks[t : t + 4]:
                copy.wait()
        downs = []
        for u in (t, t + 1):
            b = lax.rem(first + u, NBLK)
            downs.append(maps[slot_at(s_ref[SLOT_IN + b]), :])
        x = xs[t * BLOCK_ROWS : (t + 2) * BLOCK_ROWS, :]
        pair = lax.dot_general(
            jnp.concatenate(downs, axis=0), x, NT, preferred_element_type=jnp.float32
        )
        for u in range(2):
            r = pair[u * RANK : (u + 1) * RANK, u * BLOCK_ROWS : (u + 1) * BLOCK_ROWS]
            k = (t + u) % HALF
            at = slice(k * BLOCK_ROWS, (k + 1) * BLOCK_ROWS)
            if t < HALF:
                keep_ref[:, at] = r
            else:
                give_ref[:, at] = r.astype(jnp.bfloat16)
    for copy in picks:
        copy.wait()


def low_part(scalars, x, pieces):
    rows, width = x.shape
    hbm = pl.BlockSpec(memory_space=pl.ANY)
    return pl.pallas_call(
        low_kernel,
        grid_spec=pltpu.PrefetchScalarGridSpec(
            num_scalar_prefetch=1,
            grid=(1,),
            in_specs=[hbm] * 9,
            out_specs=[pl.BlockSpec((RANK, rows // 2), lambda i, s: (0, 0))] * 2 + [hbm],
            scratch_shapes=[
                pltpu.VMEM((rows, width), jnp.bfloat16),
                pltpu.VMEM((OWNERS * RANK, width), jnp.bfloat16),
                pltpu.SemaphoreType.DMA((8,)),
                pltpu.SemaphoreType.DMA((NBLK,)),
                pltpu.SemaphoreType.DMA((NBLK,)),
            ],
        ),
        out_shape=[
            jax.ShapeDtypeStruct((RANK, rows // 2), jnp.float32),
            jax.ShapeDtypeStruct((RANK, rows // 2), jnp.bfloat16),
            jax.ShapeDtypeStruct((NBLK * RANK, width), jnp.bfloat16),
        ],
        compiler_params=pltpu.CompilerParams(vmem_limit_bytes=VMEM_LIMIT),
        cost_estimate=SMALL,
        name="low_part",
    )(scalars, x, *pieces)


def up_kernel(s_ref, g_ref, mine_ref, other_ref, keep_ref, give_ref, gs, acc, sem_g):
    first = s_ref[PLACE + 1] * HALF
    width = acc.shape[1]
    columns = pl.ds(pl.multiple_of(s_ref[PLACE] * width, width), width)
    load = pltpu.make_async_copy(g_ref.at[:, columns], gs, sem_g)
    load.start()
    lane = lax.broadcasted_iota(jnp.int32, (RANK, BLOCK_ROWS), 1)
    acc[...] = jnp.zeros_like(acc)
    load.wait()
    for t in range(NBLK):
        b = lax.rem(first + t, NBLK)
        at = slice((t % HALF) * BLOCK_ROWS, (t % HALF + 1) * BLOCK_ROWS)
        low = (mine_ref if t < HALF else other_ref)[:, at]
        low = jnp.where(lane < s_ref[VALID + b], low.astype(jnp.float32), 0.0).astype(jnp.bfloat16)
        g = gs[pl.ds(pl.multiple_of(b * BLOCK_ROWS, BLOCK_ROWS), BLOCK_ROWS), :]
        r = ADAPTER_SCALE * jnp.dot(low, g, preferred_element_type=jnp.float32)
        acc[slot_at(s_ref[SLOT_OUT + b]), :] = r
    keep_ref[...] = acc[: NBLK * RANK, :]
    give_ref[...] = acc[NBLK * RANK :, :]


def up_part(scalars, cotangent, mine, other, width):
    rows = cotangent.shape[0]
    half = pl.BlockSpec(mine.shape, lambda i, s: (0, 0))
    out = jax.ShapeDtypeStruct((NBLK * RANK, width), jnp.float32)
    return pl.pallas_call(
        up_kernel,
        grid_spec=pltpu.PrefetchScalarGridSpec(
            num_scalar_prefetch=1,
            grid=(1,),
            in_specs=[pl.BlockSpec(memory_space=pl.ANY), half, half],
            out_specs=[pl.BlockSpec((NBLK * RANK, width), lambda i, s: (0, 0))] * 2,
            scratch_shapes=[
                pltpu.VMEM((rows, width), jnp.bfloat16),
                pltpu.VMEM((OWNERS * RANK, width), jnp.float32),
                pltpu.SemaphoreType.DMA,
            ],
        ),
        out_shape=[out, out],
        compiler_params=pltpu.CompilerParams(vmem_limit_bytes=VMEM_LIMIT),
        cost_estimate=SMALL,
        name="up_part",
    )(scalars, cotangent, mine, other)


def input_kernel(s_ref, g_ref, back_ref, picked_ref, *refs):
    v_pieces = refs[:8]
    out_ref, gs, staged, vs, maps, outs, sem_g, sem_v, sem_a, sem_o = refs[8:]
    features = vs.shape[0]
    share = features // OWNERS
    line = v_pieces[0].shape[0]
    loads_v = [
        pltpu.make_async_copy(p, staged.at[pl.ds(k * line, line), :], sem_v.at[k])
        for k, p in enumerate(v_pieces)
    ]
    load_a = pltpu.make_async_copy(picked_ref, maps, sem_a)
    step = 2 * BLOCK_ROWS
    loads_g, stores = [], []
    for t in range(HALF):
        at = pl.ds(t * step, step)
        to = pl.ds(t * step, step)
        loads_g.append(pltpu.make_async_copy(g_ref.at[at, :], gs.at[to, :], sem_g.at[t]))
        stores.append(pltpu.make_async_copy(outs.at[to, :], out_ref.at[at, :], sem_o.at[t]))
    for copy in loads_v + loads_g[:1] + [load_a] + loads_g[1:]:
        copy.start()
    for k in range(OWNERS):
        if k % SIDE == 0:
            loads_v[k // SIDE].wait()
        to = pl.ds(pl.multiple_of(s_ref[ORDER + k] * share, share), share)
        vs[to, :] = staged[k * share : (k + 1) * share, :]
    row = lax.broadcasted_iota(jnp.int32, (BLOCK_ROWS, features), 0)
    for t in range(HALF):
        loads_g[t].wait()
        if t == 0:
            load_a.wait()
        lives, terms = [], []
        for u in range(2):
            k = 2 * t + u
            g = gs[k * BLOCK_ROWS : (k + 1) * BLOCK_ROWS, :]
            lives.append(jnp.where(row < s_ref[VALID + k], g, jnp.zeros_like(g)))
            back = back_ref[:, k * BLOCK_ROWS : (k + 1) * BLOCK_ROWS]
            down = maps[k * RANK : (k + 1) * RANK, :]
            term = lax.dot_general(back, down, TN, preferred_element_type=jnp.float32)
            terms.append(term.astype(jnp.bfloat16).astype(jnp.float32))
        live = jnp.concatenate(lives, axis=0)
        frozen = jnp.dot(live, vs[...], preferred_element_type=jnp.float32)
        for u in range(2):
            k = 2 * t + u
            outs[k * BLOCK_ROWS : (k + 1) * BLOCK_ROWS, :] = (
                frozen[u * BLOCK_ROWS : (u + 1) * BLOCK_ROWS] + terms[u]
            ).astype(jnp.bfloat16)
        stores[t].start()
    for copy in stores:
        copy.wait()


def input_part(scalars, cotangent, back, picked, v_pieces):
    rows, features = cotangent.shape
    width = v_pieces[0].shape[1]
    hbm = pl.BlockSpec(memory_space=pl.ANY)
    half = pl.BlockSpec(back.shape, lambda i, s: (0, 0))
    return pl.pallas_call(
        input_kernel,
        grid_spec=pltpu.PrefetchScalarGridSpec(
            num_scalar_prefetch=1,
            grid=(1,),
            in_specs=[hbm, half] + [hbm] * 9,
            out_specs=hbm,
            scratch_shapes=[
                pltpu.VMEM((rows, features), jnp.bfloat16),
                pltpu.VMEM((features, width), jnp.bfloat16),
                pltpu.VMEM((features, width), jnp.bfloat16),
                pltpu.VMEM((NBLK * RANK, width), jnp.bfloat16),
                pltpu.VMEM((rows, width), jnp.bfloat16),
                pltpu.SemaphoreType.DMA((HALF,)),
                pltpu.SemaphoreType.DMA((8,)),
                pltpu.SemaphoreType.DMA,
                pltpu.SemaphoreType.DMA((HALF,)),
            ],
        ),
        out_shape=jax.ShapeDtypeStruct((rows, width), jnp.bfloat16),
        compiler_params=pltpu.CompilerParams(vmem_limit_bytes=VMEM_LIMIT),
        cost_estimate=SMALL,
        name="input_part",
    )(scalars, cotangent, back, picked, *v_pieces)


def make_scalars(task_of_block, valid_block_rows, adapter_of_task):
    w = lax.axis_index("wide")
    n = lax.axis_index("narrow")
    x, y, c = w // (2 * SIDE), (w // 2) % SIDE, w % 2
    hit = task_of_block == lax.broadcasted_iota(jnp.int32, (NBLK, OWNERS), 1)
    owner = jnp.sum(jnp.where(hit, adapter_of_task[None, :], 0), axis=1)
    ox, oy, oc = owner // (2 * SIDE), (owner // 2) % SIDE, owner % 2
    dx, dy = (x - ox) % SIDE, (y - oy) % SIDE
    i, j = jnp.where(oc == 0, dy, dx), jnp.where(oc == 0, dx, dy)
    side = (oc + c) % 2 * (SIDE * SIDE)
    slot_in = side + i * SIDE + j
    slot_out = side + (-i) % SIDE * SIDE + (-j) % SIDE
    k = lax.broadcasted_iota(jnp.int32, (OWNERS, 1), 0)[:, 0]
    kc = (k // (SIDE * SIDE) + c) % 2
    ki, kj = (k // SIDE) % SIDE, k % SIDE
    kx = (x - jnp.where(kc == 0, kj, ki)) % SIDE
    ky = (y - jnp.where(kc == 0, ki, kj)) % SIDE
    order = (kx * SIDE + ky) * 2 + kc
    spot = lax.broadcasted_iota(jnp.int32, (NBLK, 1), 0)[:, 0]
    place = jnp.where(spot == 0, n, n % 2)
    return jnp.concatenate([slot_in, slot_out, valid_block_rows, place, order])


def body(
    inputs,
    cotangent,
    value_matrix,
    adapter_down_maps,
    adapter_up_maps,
    task_of_block,
    valid_block_rows,
    adapter_of_task,
):
    scalars = make_scalars(task_of_block, valid_block_rows, adapter_of_task)
    up_own = adapter_up_maps[0]
    down_own = adapter_down_maps[0].T
    value_own = value_matrix.T

    got = gather_short(down_own)
    other = pair_step(up_own)
    other, got, scalars = tie(other, got, scalars)
    down_line = jnp.concatenate([down_own, got[1], got[2], got[3]], axis=0)
    down_pieces = gather_second(down_line)
    up_full = widen(up_own, other, 1)
    for q in (2, 4):
        up_full = widen(up_full, narrow_send(up_full, lambda i, q=q: i ^ q), q)
    own = jnp.concatenate([up_full, value_own], axis=0)
    own, *down_pieces = tie(own, *down_pieces)

    got = gather_short(own)
    parts = [own, got[1], got[2], got[3]]
    up_line = jnp.concatenate([p[:RANK] for p in parts], axis=0)
    down_pieces = down_pieces + [swap_cores(p) for p in down_pieces]
    low_keep, low_give, picked = low_part(scalars, inputs, down_pieces)
    total = add_all(low_keep, [pair_step(low_give)])
    total, up_line, parts = tie(total, up_line, parts)

    up_pieces = gather_second(up_line)
    low_mine = exchange(exchange(total, 2), 4).astype(jnp.bfloat16)
    up_first = swap_cores(up_line)
    low_mine, parts, up_first, *up_pieces = tie(low_mine, parts, up_first, *up_pieces)

    low_other = pair_step(low_mine)
    up_pieces = up_pieces + [up_first] + [swap_cores(p) for p in up_pieces[1:]]
    value_line = jnp.concatenate([p[RANK:] for p in parts], axis=0)
    low_other, value_line, *up_pieces = tie(low_other, value_line, *up_pieces)

    value_pieces = gather_second(value_line)
    back, down_keep, down_give = back_part(scalars, cotangent, inputs, up_pieces)
    low_other, down_keep, down_give, value_pieces = tie(
        low_other, down_keep, down_give, value_pieces
    )

    down_got = swap_cores(down_give)
    up_keep, up_give = up_part(scalars, cotangent, low_mine, low_other, up_own.shape[1])
    up_got = swap_cores(up_give)
    value_pieces = value_pieces + [swap_cores(p) for p in value_pieces]
    up_keep, up_got, down_keep, down_got, value_pieces = tie(
        up_keep, up_got, down_keep, down_got, value_pieces
    )

    downs = [
        k.astype(jnp.float32) + g.astype(jnp.float32)
        for k, g in zip(split_rows(down_keep), split_rows(down_got))
    ]
    ups = [k + g for k, g in zip(split_rows(up_keep), split_rows(up_got))]
    down_line, up_line = reduce_lines(downs, ups, long_axis)
    input_gradient = input_part(scalars, cotangent, back, picked, value_pieces)
    down_line, up_line, input_gradient = tie(down_line, up_line, input_gradient)

    down_grad, up_grad = reduce_lines(split_rows(down_line), split_rows(up_line), short_axis)
    return input_gradient, down_grad.T[None], up_grad[None]


def solution(mesh):
    return jax.shard_map(
        body,
        mesh=mesh,
        in_specs=(
            P("wide", "narrow"),
            P("wide", None),
            P("narrow", "wide"),
            P("wide", "narrow", None),
            P("wide", None, "narrow"),
            P("wide", None),
            P("wide"),
            P(),
        ),
        out_specs=(P("wide", "narrow"), P("wide", "narrow", None), P("wide", None, "narrow")),
        check_vma=False,
    )
```

```python
import jax
import jax.numpy as jnp
from jax import lax
from jax.experimental import pallas as pl
from jax.experimental.pallas import tpu as pltpu
from jax.sharding import PartitionSpec as P

BLOCK_ROWS = 128
ADAPTER_SCALE = 2.0
RANK = 64
SIDE = 4
NBLK = 16
OWNERS = 32
DEPTH = 8
HALF = NBLK // 2
VMEM_LIMIT = 48 * 1024 * 1024

SMALL = pl.CostEstimate(flops=1, bytes_accessed=1, transcendentals=0)

NT = (((1,), (1,)), ((), ()))
TN = (((0,), (0,)), ((), ()))

SLOT_IN, SLOT_OUT, VALID, PLACE, ORDER, SCALARS = 0, 16, 32, 48, 64, 96


def wide_index(x, y, c):
    return ((x % SIDE) * SIDE + (y % SIDE)) * 2 + c


def short_axis(d):
    return [
        (wide_index(x, y, c), wide_index(x + d, y, c) if c == 0 else wide_index(x, y + d, c))
        for x in range(SIDE)
        for y in range(SIDE)
        for c in range(2)
    ]


def long_axis(d):
    return [
        (wide_index(x, y, c), wide_index(x, y + d, c) if c == 0 else wide_index(x + d, y, c))
        for x in range(SIDE)
        for y in range(SIDE)
        for c in range(2)
    ]


def swap_cores(v):
    return lax.ppermute(v, "wide", [(w, w ^ 1) for w in range(OWNERS)])


def tie(*values):
    return lax.optimization_barrier(values)


def shift(v, axis, d):
    return lax.ppermute(v, "wide", axis(d))


def gather_short(own):
    return {d: shift(own, short_axis, d) for d in (1, 3, 2)}


def widen(own, other, q):
    late = (lax.axis_index("narrow") // q) % 2 == 1
    return jnp.concatenate([jnp.where(late, other, own), jnp.where(late, own, other)], axis=1)


def gather_second(line):
    got = {d: shift(line, long_axis, d) for d in (1, 3, 2)}
    return [line, got[1], got[2], got[3]]


def add_all(total, others):
    for other in others:
        total = total + other.astype(jnp.float32)
    return total


def send_line(down, up, axis, d):
    high = up.astype(jnp.bfloat16)
    rest = (up - high.astype(jnp.float32)).astype(jnp.bfloat16)
    got = shift(jnp.concatenate([down.astype(jnp.bfloat16), high, rest], axis=1), axis, d)
    width, share = down.shape[1], up.shape[1]
    got_up = got[:, width : width + share].astype(jnp.float32)
    return got[:, :width], got_up + got[:, width + share :].astype(jnp.float32)


def reduce_lines(downs, ups, axis):
    got = [send_line(downs[d], ups[d], axis, d) for d in (1, 3, 2)]
    return add_all(downs[0], [g[0] for g in got]), add_all(ups[0], [g[1] for g in got])


def split_rows(v):
    piece = v.shape[0] // SIDE
    return [v[i * piece : (i + 1) * piece] for i in range(SIDE)]


def narrow_send(v, f):
    return lax.ppermute(v, "narrow", [(i, f(i) % DEPTH) for i in range(DEPTH)])


def pair_step(v):
    return narrow_send(v, lambda i: i ^ 1)


def exchange(total, q):
    other = narrow_send(total.astype(jnp.bfloat16), lambda i: i ^ q)
    return total + other.astype(jnp.float32)


def block_at(b):
    return pl.ds(pl.multiple_of(b * BLOCK_ROWS, BLOCK_ROWS), BLOCK_ROWS)


def slot_at(slot):
    return pl.ds(pl.multiple_of(slot * RANK, RANK), RANK)


def back_kernel(s_ref, g_ref, x_ref, *refs):
    pieces, (back_ref, keep_ref, give_ref) = refs[:8], refs[8:11]
    gs, maps, xs, acc, sem_g, sem_b, sem_x, sem_o = refs[11:]
    per = pieces[0].shape[0]
    half_rows = NBLK * RANK
    loads = [
        pltpu.make_async_copy(p, maps.at[pl.ds(k * per, per), :], sem_b.at[k])
        for k, p in enumerate(pieces)
    ]
    g_loads, x_loads = [], []
    for t in range(HALF):
        at = pl.ds(2 * t * BLOCK_ROWS, 2 * BLOCK_ROWS)
        g_loads.append(pltpu.make_async_copy(g_ref.at[at, :], gs.at[at, :], sem_g.at[t]))
        x_loads.append(pltpu.make_async_copy(x_ref.at[at, :], xs.at[at, :], sem_x.at[t]))
    for copy in loads:
        copy.start()
    for t in range(HALF):
        g_loads[t].start()
        x_loads[t].start()
    acc[...] = jnp.zeros_like(acc)
    for copy in loads:
        copy.wait()
    lane = lax.broadcasted_iota(jnp.int32, (RANK, BLOCK_ROWS), 1)

    def backs(t):
        rows = slice(t * BLOCK_ROWS, (t + 2) * BLOCK_ROWS)
        ups = [maps[slot_at(s_ref[SLOT_IN + t + u]), :] for u in range(2)]
        pair = lax.dot_general(
            jnp.concatenate(ups, axis=0), gs[rows, :], NT, preferred_element_type=jnp.float32
        )
        parts = []
        for u in range(2):
            r = pair[u * RANK : (u + 1) * RANK, u * BLOCK_ROWS : (u + 1) * BLOCK_ROWS]
            r = jnp.where(lane < s_ref[VALID + t + u], ADAPTER_SCALE * r, 0.0)
            parts.append(r.astype(jnp.bfloat16))
        return parts

    def grads(t, parts):
        for u in range(2):
            b = t + u
            at = slice(b * BLOCK_ROWS, (b + 1) * BLOCK_ROWS)
            back_ref[:, at] = parts[u]
            grad = jnp.dot(parts[u], xs[at, :], preferred_element_type=jnp.float32)
            acc[slot_at(s_ref[SLOT_OUT + b]), :] = grad.astype(jnp.bfloat16)

    before = None
    for t in range(0, NBLK, 2):
        g_loads[t // 2].wait()
        if t:
            x_loads[t // 2 - 1].wait()
        parts = backs(t)
        if t:
            grads(t - 2, before)
        before = parts
    x_loads[HALF - 1].wait()
    grads(NBLK - 2, before)
    outs = [
        pltpu.make_async_copy(acc.at[pl.ds(half_rows, half_rows), :], give_ref, sem_o.at[0]),
        pltpu.make_async_copy(acc.at[pl.ds(0, half_rows), :], keep_ref, sem_o.at[1]),
    ]
    for copy in outs:
        copy.start()
    for copy in outs:
        copy.wait()


def back_part(scalars, cotangent, x, pieces):
    rows, features = cotangent.shape
    width = x.shape[1]
    hbm = pl.BlockSpec(memory_space=pl.ANY)
    out = jax.ShapeDtypeStruct((NBLK * RANK, width), jnp.bfloat16)
    return pl.pallas_call(
        back_kernel,
        grid_spec=pltpu.PrefetchScalarGridSpec(
            num_scalar_prefetch=1,
            grid=(1,),
            in_specs=[hbm] * 10,
            out_specs=[pl.BlockSpec((RANK, rows), lambda i, s: (0, 0)), hbm, hbm],
            scratch_shapes=[
                pltpu.VMEM((rows, features), jnp.bfloat16),
                pltpu.VMEM((OWNERS * RANK, features), jnp.bfloat16),
                pltpu.VMEM((rows, width), jnp.bfloat16),
                pltpu.VMEM((OWNERS * RANK, width), jnp.bfloat16),
                pltpu.SemaphoreType.DMA((HALF,)),
                pltpu.SemaphoreType.DMA((8,)),
                pltpu.SemaphoreType.DMA((HALF,)),
                pltpu.SemaphoreType.DMA((2,)),
            ],
        ),
        out_shape=[jax.ShapeDtypeStruct((RANK, rows), jnp.bfloat16), out, out],
        compiler_params=pltpu.CompilerParams(vmem_limit_bytes=VMEM_LIMIT),
        cost_estimate=pl.CostEstimate(
            flops=4 * rows * RANK * width, bytes_accessed=16 * 2**20, transcendentals=0
        ),
        name="back_part",
    )(scalars, cotangent, x, *pieces)


def low_kernel(s_ref, x_ref, *refs):
    pieces, (keep_ref, give_ref, picked_ref, xs, maps, sem_a, sem_x, sem_p) = refs[:8], refs[8:]
    per = pieces[0].shape[0]
    first = s_ref[PLACE + 1] * HALF
    loads = [
        pltpu.make_async_copy(p, maps.at[pl.ds(k * per, per), :], sem_a.at[k])
        for k, p in enumerate(pieces)
    ]
    blocks = []
    for t in range(NBLK):
        b = lax.rem(first + t, NBLK)
        at = pl.ds(pl.multiple_of(b * BLOCK_ROWS, BLOCK_ROWS), BLOCK_ROWS)
        to = pl.ds(t * BLOCK_ROWS, BLOCK_ROWS)
        blocks.append(pltpu.make_async_copy(x_ref.at[at, :], xs.at[to, :], sem_x.at[t]))
    for copy in loads + blocks:
        copy.start()
    for copy in loads:
        copy.wait()
    picks = []
    for b in range(NBLK):
        to = picked_ref.at[pl.ds(b * RANK, RANK), :]
        picks.append(
            pltpu.make_async_copy(maps.at[slot_at(s_ref[SLOT_IN + b]), :], to, sem_p.at[b])
        )
        picks[b].start()
    for t in range(0, NBLK, 2):
        if t % 4 == 0:
            for copy in blocks[t : t + 4]:
                copy.wait()
        downs = []
        for u in (t, t + 1):
            b = lax.rem(first + u, NBLK)
            downs.append(maps[slot_at(s_ref[SLOT_IN + b]), :])
        x = xs[t * BLOCK_ROWS : (t + 2) * BLOCK_ROWS, :]
        pair = lax.dot_general(
            jnp.concatenate(downs, axis=0), x, NT, preferred_element_type=jnp.float32
        )
        for u in range(2):
            r = pair[u * RANK : (u + 1) * RANK, u * BLOCK_ROWS : (u + 1) * BLOCK_ROWS]
            k = (t + u) % HALF
            at = slice(k * BLOCK_ROWS, (k + 1) * BLOCK_ROWS)
            if t < HALF:
                keep_ref[:, at] = r
            else:
                give_ref[:, at] = r.astype(jnp.bfloat16)
    for copy in picks:
        copy.wait()


def low_part(scalars, x, pieces):
    rows, width = x.shape
    hbm = pl.BlockSpec(memory_space=pl.ANY)
    return pl.pallas_call(
        low_kernel,
        grid_spec=pltpu.PrefetchScalarGridSpec(
            num_scalar_prefetch=1,
            grid=(1,),
            in_specs=[hbm] * 9,
            out_specs=[pl.BlockSpec((RANK, rows // 2), lambda i, s: (0, 0))] * 2 + [hbm],
            scratch_shapes=[
                pltpu.VMEM((rows, width), jnp.bfloat16),
                pltpu.VMEM((OWNERS * RANK, width), jnp.bfloat16),
                pltpu.SemaphoreType.DMA((8,)),
                pltpu.SemaphoreType.DMA((NBLK,)),
                pltpu.SemaphoreType.DMA((NBLK,)),
            ],
        ),
        out_shape=[
            jax.ShapeDtypeStruct((RANK, rows // 2), jnp.float32),
            jax.ShapeDtypeStruct((RANK, rows // 2), jnp.bfloat16),
            jax.ShapeDtypeStruct((NBLK * RANK, width), jnp.bfloat16),
        ],
        compiler_params=pltpu.CompilerParams(vmem_limit_bytes=VMEM_LIMIT),
        cost_estimate=SMALL,
        name="low_part",
    )(scalars, x, *pieces)


def up_kernel(s_ref, g_ref, mine_ref, other_ref, keep_ref, give_ref, gs, acc, sem_g):
    first = s_ref[PLACE + 1] * HALF
    width = acc.shape[1]
    columns = pl.ds(pl.multiple_of(s_ref[PLACE] * width, width), width)
    load = pltpu.make_async_copy(g_ref.at[:, columns], gs, sem_g)
    load.start()
    lane = lax.broadcasted_iota(jnp.int32, (RANK, BLOCK_ROWS), 1)
    acc[...] = jnp.zeros_like(acc)
    load.wait()
    for t in range(NBLK):
        b = lax.rem(first + t, NBLK)
        at = slice((t % HALF) * BLOCK_ROWS, (t % HALF + 1) * BLOCK_ROWS)
        low = (mine_ref if t < HALF else other_ref)[:, at]
        low = jnp.where(lane < s_ref[VALID + b], low.astype(jnp.float32), 0.0).astype(jnp.bfloat16)
        g = gs[pl.ds(pl.multiple_of(b * BLOCK_ROWS, BLOCK_ROWS), BLOCK_ROWS), :]
        r = ADAPTER_SCALE * jnp.dot(low, g, preferred_element_type=jnp.float32)
        acc[slot_at(s_ref[SLOT_OUT + b]), :] = r
    keep_ref[...] = acc[: NBLK * RANK, :]
    give_ref[...] = acc[NBLK * RANK :, :]


def up_part(scalars, cotangent, mine, other, width):
    rows = cotangent.shape[0]
    half = pl.BlockSpec(mine.shape, lambda i, s: (0, 0))
    out = jax.ShapeDtypeStruct((NBLK * RANK, width), jnp.float32)
    return pl.pallas_call(
        up_kernel,
        grid_spec=pltpu.PrefetchScalarGridSpec(
            num_scalar_prefetch=1,
            grid=(1,),
            in_specs=[pl.BlockSpec(memory_space=pl.ANY), half, half],
            out_specs=[pl.BlockSpec((NBLK * RANK, width), lambda i, s: (0, 0))] * 2,
            scratch_shapes=[
                pltpu.VMEM((rows, width), jnp.bfloat16),
                pltpu.VMEM((OWNERS * RANK, width), jnp.float32),
                pltpu.SemaphoreType.DMA,
            ],
        ),
        out_shape=[out, out],
        compiler_params=pltpu.CompilerParams(vmem_limit_bytes=VMEM_LIMIT),
        cost_estimate=SMALL,
        name="up_part",
    )(scalars, cotangent, mine, other)


def input_kernel(s_ref, g_ref, back_ref, picked_ref, *refs):
    v_pieces = refs[:8]
    out_ref, gs, staged, vs, maps, outs, sem_g, sem_v, sem_a, sem_o = refs[8:]
    features = vs.shape[0]
    share = features // OWNERS
    line = v_pieces[0].shape[0]
    loads_v = [
        pltpu.make_async_copy(p, staged.at[pl.ds(k * line, line), :], sem_v.at[k])
        for k, p in enumerate(v_pieces)
    ]
    load_a = pltpu.make_async_copy(picked_ref, maps, sem_a)
    step = 2 * BLOCK_ROWS
    loads_g, stores = [], []
    for t in range(HALF):
        at = pl.ds(t * step, step)
        to = pl.ds(t * step, step)
        loads_g.append(pltpu.make_async_copy(g_ref.at[at, :], gs.at[to, :], sem_g.at[t]))
        stores.append(pltpu.make_async_copy(outs.at[to, :], out_ref.at[at, :], sem_o.at[t]))
    for copy in loads_v + loads_g[:1] + [load_a] + loads_g[1:]:
        copy.start()
    for k in range(OWNERS):
        if k % SIDE == 0:
            loads_v[k // SIDE].wait()
        to = pl.ds(pl.multiple_of(s_ref[ORDER + k] * share, share), share)
        vs[to, :] = staged[k * share : (k + 1) * share, :]
    row = lax.broadcasted_iota(jnp.int32, (BLOCK_ROWS, features), 0)
    for t in range(HALF):
        loads_g[t].wait()
        if t == 0:
            load_a.wait()
        lives, terms = [], []
        for u in range(2):
            k = 2 * t + u
            g = gs[k * BLOCK_ROWS : (k + 1) * BLOCK_ROWS, :]
            lives.append(jnp.where(row < s_ref[VALID + k], g, jnp.zeros_like(g)))
            back = back_ref[:, k * BLOCK_ROWS : (k + 1) * BLOCK_ROWS]
            down = maps[k * RANK : (k + 1) * RANK, :]
            term = lax.dot_general(back, down, TN, preferred_element_type=jnp.float32)
            terms.append(term.astype(jnp.bfloat16).astype(jnp.float32))
        live = jnp.concatenate(lives, axis=0)
        frozen = jnp.dot(live, vs[...], preferred_element_type=jnp.float32)
        for u in range(2):
            k = 2 * t + u
            outs[k * BLOCK_ROWS : (k + 1) * BLOCK_ROWS, :] = (
                frozen[u * BLOCK_ROWS : (u + 1) * BLOCK_ROWS] + terms[u]
            ).astype(jnp.bfloat16)
        stores[t].start()
    for copy in stores:
        copy.wait()


def input_part(scalars, cotangent, back, picked, v_pieces):
    rows, features = cotangent.shape
    width = v_pieces[0].shape[1]
    hbm = pl.BlockSpec(memory_space=pl.ANY)
    half = pl.BlockSpec(back.shape, lambda i, s: (0, 0))
    return pl.pallas_call(
        input_kernel,
        grid_spec=pltpu.PrefetchScalarGridSpec(
            num_scalar_prefetch=1,
            grid=(1,),
            in_specs=[hbm, half] + [hbm] * 9,
            out_specs=hbm,
            scratch_shapes=[
                pltpu.VMEM((rows, features), jnp.bfloat16),
                pltpu.VMEM((features, width), jnp.bfloat16),
                pltpu.VMEM((features, width), jnp.bfloat16),
                pltpu.VMEM((NBLK * RANK, width), jnp.bfloat16),
                pltpu.VMEM((rows, width), jnp.bfloat16),
                pltpu.SemaphoreType.DMA((HALF,)),
                pltpu.SemaphoreType.DMA((8,)),
                pltpu.SemaphoreType.DMA,
                pltpu.SemaphoreType.DMA((HALF,)),
            ],
        ),
        out_shape=jax.ShapeDtypeStruct((rows, width), jnp.bfloat16),
        compiler_params=pltpu.CompilerParams(vmem_limit_bytes=VMEM_LIMIT),
        cost_estimate=SMALL,
        name="input_part",
    )(scalars, cotangent, back, picked, *v_pieces)


def make_scalars(task_of_block, valid_block_rows, adapter_of_task):
    w = lax.axis_index("wide")
    n = lax.axis_index("narrow")
    x, y, c = w // (2 * SIDE), (w // 2) % SIDE, w % 2
    hit = task_of_block == lax.broadcasted_iota(jnp.int32, (NBLK, OWNERS), 1)
    owner = jnp.sum(jnp.where(hit, adapter_of_task[None, :], 0), axis=1)
    ox, oy, oc = owner // (2 * SIDE), (owner // 2) % SIDE, owner % 2
    dx, dy = (x - ox) % SIDE, (y - oy) % SIDE
    i, j = jnp.where(oc == 0, dy, dx), jnp.where(oc == 0, dx, dy)
    side = (oc + c) % 2 * (SIDE * SIDE)
    slot_in = side + i * SIDE + j
    slot_out = side + (-i) % SIDE * SIDE + (-j) % SIDE
    k = lax.broadcasted_iota(jnp.int32, (OWNERS, 1), 0)[:, 0]
    kc = (k // (SIDE * SIDE) + c) % 2
    ki, kj = (k // SIDE) % SIDE, k % SIDE
    kx = (x - jnp.where(kc == 0, kj, ki)) % SIDE
    ky = (y - jnp.where(kc == 0, ki, kj)) % SIDE
    order = (kx * SIDE + ky) * 2 + kc
    spot = lax.broadcasted_iota(jnp.int32, (NBLK, 1), 0)[:, 0]
    place = jnp.where(spot == 0, n, n % 2)
    return jnp.concatenate([slot_in, slot_out, valid_block_rows, place, order])


def body(
    inputs,
    cotangent,
    value_matrix,
    adapter_down_maps,
    adapter_up_maps,
    task_of_block,
    valid_block_rows,
    adapter_of_task,
):
    scalars = make_scalars(task_of_block, valid_block_rows, adapter_of_task)
    up_own = adapter_up_maps[0]
    down_own = adapter_down_maps[0].T
    value_own = value_matrix.T

    got = gather_short(down_own)
    other = pair_step(up_own)
    other, got, scalars = tie(other, got, scalars)
    down_line = jnp.concatenate([down_own, got[1], got[2], got[3]], axis=0)
    down_pieces = gather_second(down_line)
    up_full = widen(up_own, other, 1)
    for q in (2, 4):
        up_full = widen(up_full, narrow_send(up_full, lambda i, q=q: i ^ q), q)
    own = jnp.concatenate([up_full, value_own], axis=0)
    own, *down_pieces = tie(own, *down_pieces)

    got = gather_short(own)
    parts = [own, got[1], got[2], got[3]]
    up_line = jnp.concatenate([p[:RANK] for p in parts], axis=0)
    down_pieces = down_pieces + [swap_cores(p) for p in down_pieces]
    low_keep, low_give, picked = low_part(scalars, inputs, down_pieces)
    total = add_all(low_keep, [pair_step(low_give)])
    total, up_line, parts = tie(total, up_line, parts)

    up_pieces = gather_second(up_line)
    low_mine = exchange(exchange(total, 2), 4).astype(jnp.bfloat16)
    low_mine, parts, *up_pieces = tie(low_mine, parts, *up_pieces)

    low_other = pair_step(low_mine)
    up_pieces = up_pieces + [swap_cores(p) for p in up_pieces]
    value_line = jnp.concatenate([p[RANK:] for p in parts], axis=0)
    low_other, value_line, *up_pieces = tie(low_other, value_line, *up_pieces)

    value_pieces = gather_second(value_line)
    back, down_keep, down_give = back_part(scalars, cotangent, inputs, up_pieces)
    low_other, down_keep, down_give, value_pieces = tie(
        low_other, down_keep, down_give, value_pieces
    )

    down_got = swap_cores(down_give)
    up_keep, up_give = up_part(scalars, cotangent, low_mine, low_other, up_own.shape[1])
    up_got = swap_cores(up_give)
    up_keep, up_got, down_keep, down_got, value_pieces = tie(
        up_keep, up_got, down_keep, down_got, value_pieces
    )

    downs = [
        k.astype(jnp.float32) + g.astype(jnp.float32)
        for k, g in zip(split_rows(down_keep), split_rows(down_got))
    ]
    ups = [k + g for k, g in zip(split_rows(up_keep), split_rows(up_got))]
    value_pieces = value_pieces + [swap_cores(p) for p in value_pieces]
    down_line, up_line = reduce_lines(downs, ups, long_axis)
    input_gradient = input_part(scalars, cotangent, back, picked, value_pieces)
    down_line, up_line, input_gradient = tie(down_line, up_line, input_gradient)

    down_grad, up_grad = reduce_lines(split_rows(down_line), split_rows(up_line), short_axis)
    return input_gradient, down_grad.T[None], up_grad[None]


def solution(mesh):
    return jax.shard_map(
        body,
        mesh=mesh,
        in_specs=(
            P("wide", "narrow"),
            P("wide", None),
            P("narrow", "wide"),
            P("wide", "narrow", None),
            P("wide", None, "narrow"),
            P("wide", None),
            P("wide"),
            P(),
        ),
        out_specs=(P("wide", "narrow"), P("wide", "narrow", None), P("wide", None, "narrow")),
        check_vma=False,
    )
```
